128 devices in a mesh: obs: 32 (over y, z_hi, x), vox: 4 (over z_lo, core).
Axes of the slice: x: 4, y: 4, z: 4 (z_hi: 2, z_lo: 2; z = z_hi * 2 + z_lo), core: 2. Of those that a mesh axis runs over, the one named last changes fastest.
Arguments:
- cov_slab: float32 [65536, 4096], P('vox', 'obs'), may hold values from -6 to 6
- cross_cov: bfloat16 [65536, 1024], P('vox', 'obs'), may hold values from -0.1875 to 0.1875
- ray_blocks: int32 [1024, 16], P('obs'), may hold values from 0 to 1023
- ray_coeff: float32 [1024, 1024], P('obs'), may hold values from -0.1875 to 0.1875
- region_rows: int32 [32], P('obs'), may hold values from 8 to 32, as said below
- innov_cov: float32 [1024, 1024], P('obs'), as said below
Outputs:
- new_slab: float32 [65536, 4096], P('vox', 'obs')
The draws below stay inside these ranges and needn't reach their ends.
Inputs may be any that keep to these rules, and one draw needn't show every extreme that they name: `region_rows`: every station region holds at most 32 live slots, and some region holds exactly 32. `innov_cov`: symmetric positive definite; its smallest eigenvalue is at least 2.
All inputs are finite; a program needn't handle non-finite values.
Results may differ from the reference program's by a relative error of at most 0.00068.
Values may be sent and summed in bfloat16 or wider, within the bound.
No kernel may reach another device: no remote copies, remote signals or barrier semaphores. Data moves between devices by JAX's collectives and lax.ppermute only.
A program may use at most 192 MiB of HBM per device.

```python
import jax
import jax.numpy as jnp
from jax import lax

NV = 65536
SLAB = 4096
BS = 64
NB = 16
CAP = 32
NBLK = 1024
M = 1024
N_OBS = 32


def draw_region_rows(key, part):
    key = jax.random.fold_in(key, 11)
    first, second = jax.random.split(key)
    counts = jax.random.randint(first, (N_OBS,), CAP // 4, CAP + 1)
    place = jax.random.randint(second, (), 0, N_OBS)
    return counts.at[place].set(CAP).astype(jnp.int32)


def draw_innov_cov(key, part):
    key = jax.random.fold_in(key, 23)
    first, second = jax.random.split(key)
    inner = max(M // 8, 1)
    paths = jax.random.randint(first, (M, inner), -2, 3).astype(jnp.int32)
    shared = jnp.dot(paths, paths.T, preferred_element_type=jnp.int32).astype(jnp.float32)
    strength = 0.4
    extra = jnp.exp(jax.random.uniform(second, (M,), jnp.float32, jnp.log(0.5), jnp.log(5.0)))
    eye = jnp.eye(M, dtype=jnp.float32)
    return shared * (strength / inner) + eye * (1.5 + extra)[:, None]


def touch_ends(result, stream_key, low, high):
    spot = [jax.random.randint(jax.random.fold_in(stream_key, axis), (), 0, length) for axis, length in enumerate(result.shape)]
    longest = result.shape.index(max(result.shape))
    next_to = spot[:longest] + [(spot[longest] + 1) % result.shape[longest]] + spot[longest + 1:]
    return result.at[tuple(spot)].set(low).at[tuple(next_to)].set(high)


def block_levels(key, shape, cuts, smallest, largest):
    loudness = 1.0
    for dim, parts in cuts:
        draws = jax.random.uniform(jax.random.fold_in(jax.random.fold_in(key, 6), dim), (parts,), jnp.float32, smallest / len(cuts), largest / len(cuts))
        loudness = loudness * jnp.repeat(jnp.exp(draws), shape[dim] // parts).reshape((-1,) + (1,) * (len(shape) - 1 - dim))
    return loudness


def bell_draw(own_key, shape, deviation, limit, shards=(), held_as=jnp.bfloat16):
    loudness = block_levels(own_key, shape, shards, -0.22, 0.18) if shards else 1.0
    values = jax.random.normal(own_key, shape, jnp.float32) * deviation * loudness
    return jnp.minimum(jnp.maximum(values, -limit), limit).astype(held_as)


def setup_inputs(seed: int = 0) -> dict:
    splits = jax.random.split(jax.random.key(seed), 7)
    cov_slab = bell_draw(splits[0], (NV, SLAB), 1.0, 6.0, ((0, 4), (1, 32)), jnp.float32)
    cross_cov = bell_draw(splits[1], (NV, M), M ** -0.5, 0.1875, ((0, 4), (1, 32)))
    ray_blocks = touch_ends(jax.random.randint(splits[2], (M, NB), 0, NBLK), jax.random.fold_in(splits[2], 1), 0, NBLK - 1).astype(jnp.int32)
    ray_coeff = bell_draw(splits[3], (M, NB * BS), (NB * BS) ** -0.5, 0.1875, ((0, 32),), jnp.float32)
    region_rows = draw_region_rows(jax.random.fold_in(splits[6], 71), 0)
    innov_cov = draw_innov_cov(jax.random.fold_in(splits[6], 71), 0)
    return {"cov_slab": cov_slab, "cross_cov": cross_cov, "ray_blocks": ray_blocks, "ray_coeff": ray_coeff, "region_rows": region_rows, "innov_cov": innov_cov}


def reference(cov_slab, cross_cov, ray_blocks, ray_coeff, region_rows, innov_cov):
    slot_index = jnp.arange(M, dtype=jnp.int32)
    live_slots = (slot_index % CAP < jnp.repeat(region_rows, CAP)).astype(jnp.float32)
    weights = (ray_coeff * live_slots[:, None]).reshape(M, NB, BS)
    blocked = cov_slab.reshape(NBLK, BS, SLAB)

    def one_row(packed):
        index_row, weight_row = packed
        picked = blocked[index_row]
        return jnp.einsum('nb,nbc->c', weight_row, picked, precision=lax.Precision.HIGHEST)
    predicted = lax.map(one_row, (ray_blocks, weights))
    factor = jnp.linalg.cholesky(innov_cov)
    middle = lax.linalg.triangular_solve(factor, predicted, left_side=True, lower=True)
    solved = lax.linalg.triangular_solve(factor, middle, left_side=True, lower=True, transpose_a=True)
    solved = solved.astype(jnp.bfloat16)
    return cov_slab - jnp.dot(cross_cov.astype(jnp.float32), solved.astype(jnp.float32), preferred_element_type=jnp.float32)
```

```python
import functools

import jax
import jax.numpy as jnp
from jax import lax
from jax.experimental import pallas as pl
from jax.experimental.pallas import tpu as pltpu
from jax.sharding import PartitionSpec as P

F32 = jnp.float32
BF16 = jnp.bfloat16
VMEM_LIMIT = 60 * 1024 * 1024


def halves(x):
    high = x.astype(BF16)
    return high, (x - high.astype(F32)).astype(BF16)


def dot(a, b):
    return jnp.dot(a, b, preferred_element_type=F32)


def dot_split(a, b):
    ah, al = halves(a)
    bh, bl = halves(b)
    return dot(ah, bh) + (dot(ah, bl) + dot(al, bh))


def predict_kernel(place_ref, block_ref, weight_ref, cov_ref, out_ref, dense, cov_split, *, tile, crossing, block):
    step = pl.program_id(0)
    rows, columns = cov_ref.shape
    pairs = rows // (2 * block)
    deep = 2 * 2 * block
    quads = rows // deep
    lane = lax.broadcasted_iota(jnp.int32, (8, 2 * block), 1)
    sub = lax.broadcasted_iota(jnp.int32, (8, 2 * block), 0)
    upper = (lane >= block).astype(jnp.int32)

    @pl.when(step == 0)
    def _():
        def clear(i, c):
            dense[i] = jnp.zeros_like(dense[i])
            return c

        lax.fori_loop(0, pairs, clear, 0)

        def split(i, c):
            high, low = halves(cov_ref[pl.ds(pl.multiple_of(i * deep, deep), deep), :])
            cov_split[i, :, :columns] = high
            cov_split[i, :, columns:] = low
            return c

        lax.fori_loop(0, quads, split, 0)

    def scatter(group, c):
        row = pl.multiple_of(group * 8, 8)
        first = (step * tile + row) * crossing
        blocks = block_ref[pl.ds(row, 8), :] & 1
        for n in range(crossing):
            if n % 2 == 0:
                plain = weight_ref[pl.ds(row, 8), pl.ds(n * block, 2 * block)]
                turned = pltpu.roll(plain, block, 1)
                both = jnp.where(upper == 0, plain, turned)
            else:
                both = jnp.where(upper == 0, turned, plain)
            half = blocks[:, n : n + 1] == upper
            for i in range(8):
                where = place_ref[first + i * crossing + n]
                pltpu.store(dense.at[where, pl.ds(row, 8), :], both, mask=half & (sub == i))
        return c

    lax.fori_loop(0, tile // 8, scatter, 0)
    out_ref[...] = jnp.zeros_like(out_ref)
    together = 4

    def multiply(i, c):
        total = jnp.zeros((tile, 2 * columns), F32)
        small = jnp.zeros((tile, columns), F32)
        for k in range(together):
            q = i * together + k
            wide = jnp.concatenate([dense[2 * q], dense[2 * q + 1]], axis=1)
            high, low = halves(wide)
            total = total + dot(high, cov_split[q])
            small = small + dot(low, cov_split[q, :, :columns])
            dense[2 * q] = jnp.zeros((tile, 2 * block), F32)
            dense[2 * q + 1] = jnp.zeros((tile, 2 * block), F32)
        out_ref[...] += total[:, :columns] + (total[:, columns:] + small)
        return c

    lax.fori_loop(0, quads // together, multiply, 0)


def predict(place, blocks, weights, cov_slab, crossing, block):
    slots = blocks.shape[0]
    rows, columns = cov_slab.shape
    tile = 256
    return pl.pallas_call(
        functools.partial(predict_kernel, tile=tile, crossing=crossing, block=block),
        grid=(slots // tile,),
        in_specs=[
            pl.BlockSpec(memory_space=pltpu.SMEM),
            pl.BlockSpec((tile, crossing), lambda i: (i, 0)),
            pl.BlockSpec((tile, crossing * block), lambda i: (i, 0)),
            pl.BlockSpec(memory_space=pltpu.VMEM),
        ],
        out_specs=pl.BlockSpec((tile, columns), lambda i: (i, 0)),
        out_shape=jax.ShapeDtypeStruct((slots, columns), F32),
        scratch_shapes=[
            pltpu.VMEM((rows // (2 * block) + 1, tile, 2 * block), F32),
            pltpu.VMEM((rows // (4 * block), 4 * block, 2 * columns), BF16),
        ],
        compiler_params=pltpu.CompilerParams(vmem_limit_bytes=VMEM_LIMIT),
        cost_estimate=pl.CostEstimate(
            flops=6 * slots * rows * columns, bytes_accessed=rows * columns * 4, transcendentals=0
        ),
        name="predict",
    )(place, blocks, weights, cov_slab)


def strip_sweep(strip):
    sub = lax.broadcasted_iota(jnp.int32, strip.shape, 0)
    lane = lax.broadcasted_iota(jnp.int32, strip.shape, 1)
    cols = [jnp.broadcast_to(strip[:, j : j + 1], strip.shape) for j in range(8)]
    for p in range(8):
        mine = sub == p
        inv = 1.0 / jnp.broadcast_to(cols[p][p : p + 1, :], strip.shape)
        strip = jnp.where(lane == p, jnp.where(mine, 1.0, 0.0), strip)
        head = jnp.broadcast_to(strip[p : p + 1, :], strip.shape) * inv
        strip = jnp.where(mine, head, strip - cols[p] * head)
        for j in range(p + 1, 8):
            top = jnp.broadcast_to(cols[j][p : p + 1, :], strip.shape) * inv
            cols[j] = jnp.where(mine, top, cols[j] - cols[p] * top)
    return jnp.where(lane < 8, -strip, strip)


def small_sweep(block):
    size = block.shape[0]
    lane = lax.broadcasted_iota(jnp.int32, block.shape, 1)

    def group(_, s):
        top = strip_sweep(s[:8, :])
        rest = jnp.where(lane < 8, 0.0, s)
        for j in range(8):
            rest = rest - s[:, j : j + 1] * top[j : j + 1, :]
        new = jnp.concatenate([rest[8:, :], top], axis=0)
        return pltpu.roll(new, size - 8, 1)

    return lax.fori_loop(0, size // 8, group, block)


def inverse_kernel(a_ref, m_ref, left, right, pivot, *, size):
    n = a_ref.shape[0]
    m_ref[...] = a_ref[...]

    def sweep(k, c):
        at = pl.ds(pl.multiple_of(k * size, size), size)
        minus = small_sweep(m_ref[at, at])
        pivot[...] = dot_split(minus, m_ref[at, :]) * -1.0
        pivot[:, at] = minus
        high, low = halves(m_ref[:, at])
        left[:, :size] = high
        left[:, size:] = low
        m_ref[:, at] = jnp.zeros((n, size), F32)
        high, low = halves(pivot[...])
        right[:size, :] = high
        right[size : 2 * size, :] = high
        right[2 * size :, :] = low

        def update(i, c):
            here = pl.ds(pl.multiple_of(i * size, size), size)
            both = left[here, :]
            product = dot(both, right[: 2 * size, :]) + dot(both[:, :size], right[2 * size :, :])
            m_ref[here, :] = m_ref[here, :] - product
            return c

        lax.fori_loop(0, n // size, update, 0)
        m_ref[at, :] = pivot[...]
        return c

    lax.fori_loop(0, n // size, sweep, 0)


def minus_inverse(a):
    n = a.shape[0]
    size = 128
    return pl.pallas_call(
        functools.partial(inverse_kernel, size=size),
        in_specs=[pl.BlockSpec(memory_space=pltpu.VMEM)],
        out_specs=pl.BlockSpec(memory_space=pltpu.VMEM),
        out_shape=jax.ShapeDtypeStruct((n, n), F32),
        scratch_shapes=[
            pltpu.VMEM((n, 2 * size), BF16),
            pltpu.VMEM((3 * size, n), BF16),
            pltpu.VMEM((size, n), F32),
        ],
        compiler_params=pltpu.CompilerParams(vmem_limit_bytes=VMEM_LIMIT),
        cost_estimate=pl.CostEstimate(flops=60 * n * n * n, bytes_accessed=8 * n * n, transcendentals=0),
        name="minus_inverse",
    )(a)


def update_kernel(minus_ref, predicted_ref, cross_ref, cov_ref, out_ref, solved):
    @pl.when(pl.program_id(0) == 0)
    def _():
        turned = predicted_ref[...].T
        solved[...] = (-dot_split(turned, minus_ref[...])).astype(BF16)

    product = dot(solved[...], cross_ref[...])
    out_ref[...] = cov_ref[...] - product.T


def update(minus, predicted, cross_turned, cov_slab):
    rows, columns = cov_slab.shape
    n = minus.shape[0]
    tile = 1024
    return pl.pallas_call(
        update_kernel,
        grid=(rows // tile,),
        in_specs=[
            pl.BlockSpec(memory_space=pltpu.VMEM),
            pl.BlockSpec(memory_space=pltpu.VMEM),
            pl.BlockSpec((n, tile), lambda i: (0, i)),
            pl.BlockSpec((tile, columns), lambda i: (i, 0)),
        ],
        out_specs=pl.BlockSpec((tile, columns), lambda i: (i, 0)),
        out_shape=jax.ShapeDtypeStruct((rows, columns), F32),
        scratch_shapes=[pltpu.VMEM((columns, n), BF16)],
        compiler_params=pltpu.CompilerParams(vmem_limit_bytes=VMEM_LIMIT),
        cost_estimate=pl.CostEstimate(
            flops=2 * rows * columns * n, bytes_accessed=rows * (2 * n + 8 * columns), transcendentals=0
        ),
        name="downdate",
    )(minus, predicted, cross_turned, cov_slab)


def merged(ray_blocks, weights):
    slots, crossing = ray_blocks.shape
    same = ray_blocks[:, :, None] == ray_blocks[:, None, :]
    order = jnp.arange(crossing, dtype=jnp.int32)
    first = ~jnp.any(same & (order[None, None, :] < order[None, :, None]), axis=2)
    parts = weights.reshape(slots, crossing, -1)
    total = jnp.sum(jnp.where(same[:, :, :, None], parts[:, None, :, :], 0.0), axis=2)
    return jnp.where(first, ray_blocks, -1), total.reshape(weights.shape)


def shards(cov_slab, cross_cov, ray_blocks, ray_coeff, region_rows, innov_cov):
    local_rows, columns = cov_slab.shape
    slot_count, crossing = ray_blocks.shape
    block_size = ray_coeff.shape[1] // crossing
    local_blocks = local_rows // block_size
    live = jnp.arange(slot_count, dtype=jnp.int32) < region_rows[0]
    weights = jnp.where(live[:, None], ray_coeff, 0.0)
    blocks, weights = merged(ray_blocks, weights)
    first_block = lax.axis_index("vox") * local_blocks
    blocks = lax.all_gather(blocks, "obs", axis=0, tiled=True)
    weights = lax.all_gather(weights, "obs", axis=0, tiled=True)
    local = blocks - first_block
    inside = (local >= 0) & (local < local_blocks) & (blocks >= 0)
    place = jnp.where(inside, local // 2, local_blocks // 2).reshape(-1)
    predicted = lax.psum(predict(place, blocks, weights, cov_slab, crossing, block_size), "vox")
    whole_innov = lax.all_gather(innov_cov, "obs", axis=0, tiled=True)
    minus = minus_inverse(whole_innov)
    cross_turned = lax.all_gather(cross_cov.T, "obs", axis=0, tiled=True)
    return update(minus, predicted, cross_turned, cov_slab)


def solution(mesh):
    placed = (
        P("vox", "obs"),
        P("vox", "obs"),
        P("obs", None),
        P("obs", None),
        P("obs"),
        P("obs", None),
    )
    return jax.shard_map(
        shards, mesh=mesh, in_specs=placed, out_specs=P("vox", "obs"), check_vma=False
    )
```

```python
import functools
import math

import jax
import jax.numpy as jnp
from jax import lax
from jax.experimental import pallas as pl
from jax.experimental.pallas import tpu as pltpu
from jax.sharding import PartitionSpec as P

F32 = jnp.float32
BF16 = jnp.bfloat16
VMEM_LIMIT = 60 * 1024 * 1024


def halves(x):
    high = x.astype(BF16)
    return high, (x - high.astype(F32)).astype(BF16)


def dot(a, b):
    return jnp.dot(a, b, preferred_element_type=F32)


def dot_split(a, b):
    ah, al = halves(a)
    bh, bl = halves(b)
    return dot(ah, bh) + (dot(ah, bl) + dot(al, bh))


def split_kernel(cov_ref, out_ref):
    columns = cov_ref.shape[1]
    high, low = halves(cov_ref[...])
    out_ref[:, :columns] = high
    out_ref[:, columns:] = low


def split_slab(cov_slab):
    rows, columns = cov_slab.shape
    tile = 2048
    return pl.pallas_call(
        split_kernel,
        grid=(rows // tile,),
        in_specs=[pl.BlockSpec((tile, columns), lambda i: (i, 0))],
        out_specs=pl.BlockSpec((tile, 2 * columns), lambda i: (i, 0)),
        out_shape=jax.ShapeDtypeStruct((rows, 2 * columns), BF16),
        compiler_params=pltpu.CompilerParams(vmem_limit_bytes=VMEM_LIMIT),
        cost_estimate=pl.CostEstimate(flops=4 * rows * columns, bytes_accessed=8 * rows * columns, transcendentals=0),
        name="split",
    )(cov_slab)


def predict_kernel(place_ref, slots_ref, split_ref, out_ref, dense, *, tile, crossing, block):
    step = pl.program_id(0)
    rows, columns = split_ref.shape
    columns = columns // 2
    pairs = rows // (2 * block)
    deep = 2 * 2 * block
    quads = rows // deep
    lane = lax.broadcasted_iota(jnp.int32, (8, 2 * block), 1)
    sub = lax.broadcasted_iota(jnp.int32, (8, 2 * block), 0)
    upper = (lane >= block).astype(jnp.int32)

    @pl.when(step == 0)
    def _():
        def clear(i, c):
            dense[i] = jnp.zeros_like(dense[i])
            return c

        lax.fori_loop(0, pairs, clear, 0)

    def scatter(group, c):
        row = pl.multiple_of(group * 8, 8)
        first = (step * tile + row) * crossing
        blocks = slots_ref[pl.ds(row, 8), crossing * block :].astype(jnp.int32) & 1
        for n in range(crossing):
            if n % 2 == 0:
                plain = slots_ref[pl.ds(row, 8), pl.ds(n * block, 2 * block)]
                turned = pltpu.roll(plain, block, 1)
                both = jnp.where(upper == 0, plain, turned)
            else:
                both = jnp.where(upper == 0, turned, plain)
            half = blocks[:, n : n + 1] == upper
            for i in range(8):
                where = place_ref[first + i * crossing + n]
                pltpu.store(dense.at[where, pl.ds(row, 8), :], both, mask=half & (sub == i))
        return c

    lax.fori_loop(0, tile // 8, scatter, 0)
    out_ref[...] = jnp.zeros_like(out_ref)
    together = 8

    def multiply(i, c):
        wide_sum = jnp.zeros((tile, 2 * columns), F32)
        small = jnp.zeros((tile, columns), F32)
        for k in range(together):
            q = i * together + k
            here = pl.ds(pl.multiple_of(q * deep, deep), deep)
            wide = jnp.concatenate([dense[2 * q], dense[2 * q + 1]], axis=1)
            high, low = halves(wide)
            wide_sum = wide_sum + dot(high, split_ref[here, :])
            small = small + dot(low, split_ref[here, :columns])
            dense[2 * q] = jnp.zeros((tile, 2 * block), F32)
            dense[2 * q + 1] = jnp.zeros((tile, 2 * block), F32)
        out_ref[...] += wide_sum[:, :columns] + (wide_sum[:, columns:] + small)
        return c

    lax.fori_loop(0, quads // together, multiply, 0)


def predict(slots, slab_split, first_block, local_blocks, crossing, block):
    count, width = slots.shape
    rows, columns = slab_split.shape
    columns = columns // 2
    tile = 256
    lanes = crossing * block
    blocks = slots[:, lanes : lanes + crossing].astype(jnp.int32)
    local = blocks - first_block
    inside = (local >= 0) & (local < local_blocks) & (blocks >= 0)
    place = jnp.where(inside, local // 2, local_blocks // 2).reshape(-1)
    return pl.pallas_call(
        functools.partial(predict_kernel, tile=tile, crossing=crossing, block=block),
        grid_spec=pltpu.PrefetchScalarGridSpec(
            num_scalar_prefetch=1,
            grid=(count // tile,),
            in_specs=[
                pl.BlockSpec((tile, width), lambda i, place: (i, 0)),
                pl.BlockSpec(memory_space=pltpu.VMEM),
            ],
            out_specs=pl.BlockSpec((tile, columns), lambda i, place: (i, 0)),
            scratch_shapes=[pltpu.VMEM((rows // (2 * block) + 1, tile, 2 * block), F32)],
        ),
        out_shape=jax.ShapeDtypeStruct((count, columns), F32),
        compiler_params=pltpu.CompilerParams(vmem_limit_bytes=VMEM_LIMIT),
        cost_estimate=pl.CostEstimate(
            flops=12 * count * rows * columns, bytes_accessed=rows * columns * 4, transcendentals=0
        ),
        name="predict",
    )(place, slots, slab_split)


def sweep_rows(rows, first):
    sub = lax.broadcasted_iota(jnp.int32, rows.shape, 0)
    lane = lax.broadcasted_iota(jnp.int32, rows.shape, 1) - first
    cols = [jnp.broadcast_to(rows[:, first + j : first + j + 1], rows.shape) for j in range(8)]

    def row(v, p):
        return jnp.broadcast_to(v[p : p + 1, :], rows.shape)

    out = rows
    for p in range(0, 8, 2):
        q = p + 1
        a, b, d = row(cols[p], p), row(cols[q], p), row(cols[q], q)
        inv = 1.0 / (a * d - b * b)
        a, b, d = a * inv, b * inv, d * inv
        out = jnp.where((lane == p) | (lane == q), jnp.where(sub == lane, 1.0, 0.0), out)

        def eliminate(v):
            at_p, at_q = row(v, p), row(v, q)
            new_p = d * at_p - b * at_q
            new_q = a * at_q - b * at_p
            rest = v - cols[p] * new_p - cols[q] * new_q
            return jnp.where(sub == p, new_p, jnp.where(sub == q, new_q, rest))

        out = eliminate(out)
        cols = [eliminate(col) if j > q else col for j, col in enumerate(cols)]
    return jnp.where((lane >= 0) & (lane < 8), -out, out)


def small_sweep(block):
    size = block.shape[0]
    strip = 16
    lanes = lax.broadcasted_iota(jnp.int32, (8, size), 1)
    all_lanes = lax.broadcasted_iota(jnp.int32, (size, size), 1)
    for base in range(0, size, strip):
        rows = [block[at : at + 8, :] for at in range(base, base + strip, 8)]
        for g in range(strip // 8):
            first = base + 8 * g
            top = sweep_rows(rows[g], first)
            pivots = (lanes >= first) & (lanes < first + 8)
            for e in range(strip // 8):
                if e != g:
                    rest = jnp.where(pivots, 0.0, rows[e])
                    for j in range(8):
                        rest = rest - rows[e][:, first + j : first + j + 1] * top[j : j + 1, :]
                    rows[e] = rest
            rows[g] = top
        middle = jnp.concatenate(rows, axis=0)
        above = [jnp.zeros((base, size), F32)] if base else []
        below = [jnp.zeros((size - base - strip, size), F32)] if base + strip < size else []
        high, low = halves(jnp.concatenate(above + [middle] + below, axis=0))
        block_high, block_low = halves(block)
        keep = jnp.where((all_lanes >= base) & (all_lanes < base + strip), 0.0, block)
        new = keep - (
            dot(jnp.concatenate([block_high, block_low], axis=1), jnp.concatenate([high, high], axis=0))
            + dot(block_high, low)
        )
        above = [new[:base]] if base else []
        below = [new[base + strip :]] if base + strip < size else []
        block = jnp.concatenate(above + [middle] + below, axis=0)
    return block


def inverse_kernel(core_ref, own_ref, other_ref, m_ref, left, right, pivot, *, size):
    n = m_ref.shape[0]
    regions, share, _ = own_ref.shape
    core = core_ref[0]

    def place(i, c):
        mine = pl.multiple_of((2 * i + core) * share, share)
        theirs = pl.multiple_of((2 * i + 1 - core) * share, share)
        m_ref[pl.ds(mine, share), :] = own_ref[i]
        m_ref[pl.ds(theirs, share), :] = other_ref[i]
        return c

    lax.fori_loop(0, regions, place, 0)

    def sweep(k, c):
        at = pl.ds(pl.multiple_of(k * size, size), size)
        minus = small_sweep(m_ref[at, at])
        pivot[...] = dot_split(minus, m_ref[at, :]) * -1.0
        pivot[:, at] = minus
        high, low = halves(m_ref[:, at])
        left[:, :size] = high
        left[:, size:] = low
        m_ref[:, at] = jnp.zeros((n, size), F32)
        high, low = halves(pivot[...])
        right[:size, :] = high
        right[size : 2 * size, :] = high
        right[2 * size :, :] = low
        wide = n // 2

        def update(i, c):
            here = pl.ds(pl.multiple_of(i * wide, wide), wide)
            product = dot(left[...], right[: 2 * size, here]) + dot(left[:, :size], right[2 * size :, here])
            m_ref[:, here] = m_ref[:, here] - product
            return c

        lax.fori_loop(0, n // wide, update, 0)
        m_ref[at, :] = pivot[...]
        return c

    lax.fori_loop(0, n // size, sweep, 0)


def minus_inverse(core, own, other):
    n = own.shape[2]
    size = 128
    return pl.pallas_call(
        functools.partial(inverse_kernel, size=size),
        in_specs=[pl.BlockSpec(memory_space=pltpu.SMEM)] + [pl.BlockSpec(memory_space=pltpu.VMEM)] * 2,
        out_specs=pl.BlockSpec(memory_space=pltpu.VMEM),
        out_shape=jax.ShapeDtypeStruct((n, n), F32),
        scratch_shapes=[
            pltpu.VMEM((n, 2 * size), BF16),
            pltpu.VMEM((3 * size, n), BF16),
            pltpu.VMEM((size, n), F32),
        ],
        compiler_params=pltpu.CompilerParams(vmem_limit_bytes=VMEM_LIMIT),
        cost_estimate=pl.CostEstimate(flops=60 * n * n * n, bytes_accessed=8 * n * n, transcendentals=0),
        name="minus_inverse",
    )(core, own, other)


def solve_kernel(minus_ref, predicted_ref, out_ref):
    predicted = predicted_ref[...].reshape(minus_ref.shape[0], -1)
    out_ref[...] = (-dot_split(predicted.T, minus_ref[...])).astype(BF16)


def solve_turned(minus, predicted):
    n, columns = minus.shape[0], predicted.shape[-1]
    return pl.pallas_call(
        solve_kernel,
        in_specs=[pl.BlockSpec(memory_space=pltpu.VMEM)] * 2,
        out_specs=pl.BlockSpec(memory_space=pltpu.VMEM),
        out_shape=jax.ShapeDtypeStruct((columns, n), BF16),
        compiler_params=pltpu.CompilerParams(vmem_limit_bytes=VMEM_LIMIT),
        cost_estimate=pl.CostEstimate(flops=6 * n * n * columns, bytes_accessed=4 * n * n, transcendentals=0),
        name="solve",
    )(minus, predicted)


def spread_kernel(by_x_ref, by_y_ref, out_ref):
    out_ref[0, 0] = by_x_ref[...]
    out_ref[0, 1] = by_y_ref[...]


def spread(turned):
    slots, rows = turned.shape
    width = rows // 8
    everyone = math.prod(SIZES)
    return pl.pallas_call(
        spread_kernel,
        grid=(everyone,),
        in_specs=[
            pl.BlockSpec((slots, width), lambda i: (0, i % 4)),
            pl.BlockSpec((slots, width), lambda i: (0, 4 + i // 8)),
        ],
        out_specs=pl.BlockSpec((1, 2, slots, width), lambda i: (i, 0, 0, 0)),
        out_shape=jax.ShapeDtypeStruct((everyone, 2, slots, width), turned.dtype),
        compiler_params=pltpu.CompilerParams(vmem_limit_bytes=VMEM_LIMIT),
        cost_estimate=pl.CostEstimate(flops=0, bytes_accessed=16 * slots * rows, transcendentals=0),
        name="spread",
    )(turned, turned)


def product_kernel(*refs, members):
    solved_refs, cross_ref, out_refs, stack = refs[:members], refs[members], refs[members + 1 : -1], refs[-1]
    columns = solved_refs[0].shape[0]

    @pl.when(pl.program_id(0) == 0)
    def _():
        for i, ref in enumerate(solved_refs):
            stack[i * columns : (i + 1) * columns, :] = ref[...]

    everyone, _, slots, tile = cross_ref.shape
    product = dot(stack[...], cross_ref[...].reshape(everyone * slots, tile))
    for i, ref in enumerate(out_refs):
        ref[...] = product[i * columns : (i + 1) * columns, :].astype(ref.dtype)


def products(solved, cross, half):
    members = len(solved)
    columns, n = solved[0].shape
    everyone, _, slots, width = cross.shape
    tile = 512
    return pl.pallas_call(
        functools.partial(product_kernel, members=members),
        grid=(width // tile,),
        in_specs=[pl.BlockSpec(memory_space=pltpu.VMEM)] * members
        + [pl.BlockSpec((everyone, 1, slots, tile), lambda i: (0, half, 0, i))],
        out_specs=[pl.BlockSpec((columns, tile), lambda i: (0, i))] * members,
        out_shape=[jax.ShapeDtypeStruct((columns, width), BF16 if i else F32) for i in range(members)],
        scratch_shapes=[pltpu.VMEM((members * columns, n), BF16)],
        compiler_params=pltpu.CompilerParams(vmem_limit_bytes=VMEM_LIMIT),
        cost_estimate=pl.CostEstimate(
            flops=2 * members * columns * n * width, bytes_accessed=2 * n * width, transcendentals=0
        ),
        name="products",
    )(*solved, cross)


def downdate_kernel(chunk_ref, *refs):
    product_refs, cov_ref, out_ref = refs[:-2], refs[-2], refs[-1]
    for i, ref in enumerate(product_refs):

        @pl.when(pl.program_id(0) == i)
        def _():
            out_ref[...] = cov_ref[...] - ref[...].astype(F32).T


def downdate(chunks, parts, cov_slab):
    rows, columns = cov_slab.shape
    tile = rows // len(parts)
    return pl.pallas_call(
        downdate_kernel,
        grid_spec=pltpu.PrefetchScalarGridSpec(
            num_scalar_prefetch=1,
            grid=(len(parts),),
            in_specs=[pl.BlockSpec(memory_space=pltpu.VMEM)] * len(parts)
            + [pl.BlockSpec((tile, columns), lambda i, chunk: (chunk[i], 0))],
            out_specs=pl.BlockSpec((tile, columns), lambda i, chunk: (chunk[i], 0)),
        ),
        out_shape=jax.ShapeDtypeStruct((rows, columns), F32),
        compiler_params=pltpu.CompilerParams(vmem_limit_bytes=VMEM_LIMIT),
        cost_estimate=pl.CostEstimate(flops=rows * columns, bytes_accessed=10 * rows * columns, transcendentals=0),
        name="downdate",
    )(chunks, *parts, cov_slab)


def merged(ray_blocks, weights):
    slots, crossing = ray_blocks.shape
    same = ray_blocks[:, :, None] == ray_blocks[:, None, :]
    order = jnp.arange(crossing, dtype=jnp.int32)
    first = ~jnp.any(same & (order[None, None, :] < order[None, :, None]), axis=2)
    parts = weights.reshape(slots, crossing, -1)
    total = jnp.sum(jnp.where(same[:, :, :, None], parts[:, None, :, :], 0.0), axis=2)
    return jnp.where(first, ray_blocks, -1), total.reshape(weights.shape)


SIZES = (4, 2, 4)
SWAP = [(0, 1), (1, 0), (2, 3), (3, 2)]


def steps_along(axis, distance):
    pairs = []
    for y in range(SIZES[0]):
        for z in range(SIZES[1]):
            for x in range(SIZES[2]):
                to = [y, z, x]
                to[axis] = (to[axis] + distance) % SIZES[axis]
                pairs.append(((y * SIZES[1] + z) * SIZES[2] + x, (to[0] * SIZES[1] + to[1]) * SIZES[2] + to[2]))
    return pairs


def to_all(piece):
    everyone = math.prod(SIZES)
    return lax.all_to_all(jnp.broadcast_to(piece[None], (everyone,) + piece.shape), "obs", 0, 0)


def shards(cov_slab, cross_cov, ray_blocks, ray_coeff, region_rows, innov_cov):
    local_rows, columns = cov_slab.shape
    slot_count, crossing = ray_blocks.shape
    block_size = ray_coeff.shape[1] // crossing
    local_blocks = local_rows // block_size
    everyone = math.prod(SIZES)
    device = lax.axis_index("obs")
    core = lax.axis_index("vox") % 2
    core_array = core.astype(jnp.int32).reshape(1)
    share = slot_count // 2
    start = core * share

    my_blocks = lax.dynamic_slice_in_dim(ray_blocks, start, share, 0)
    my_coeff = lax.dynamic_slice_in_dim(ray_coeff, start, share, 0)
    live = start + jnp.arange(share, dtype=jnp.int32) < region_rows[0]
    weights = jnp.where(live[:, None], my_coeff, 0.0)
    blocks, weights = merged(my_blocks, weights)
    message = jnp.concatenate([weights, jnp.pad(blocks.astype(F32), ((0, 0), (0, 128 - crossing)))], axis=1)
    own = to_all(message)

    slab_split = split_slab(cov_slab)
    send = spread(cross_cov.T)
    my_innov = lax.dynamic_slice_in_dim(innov_cov, start, share, 0)
    own, send, slab_split, my_innov = lax.optimization_barrier((own, send, slab_split, my_innov))
    innov_own = to_all(my_innov)
    other = lax.ppermute(own, "vox", SWAP)
    first_block = lax.axis_index("vox") * local_blocks
    flat = (everyone * share, -1)
    partial_own = predict(own.reshape(flat), slab_split, first_block, local_blocks, crossing, block_size)
    innov_own, send, other, partial_own = lax.optimization_barrier((innov_own, send, other, partial_own))
    cross = lax.all_to_all(send, "obs", 0, 0)
    innov_other = lax.ppermute(innov_own, "vox", SWAP)
    partial_other = predict(other.reshape(flat), slab_split, first_block, local_blocks, crossing, block_size)

    mine = partial_own + lax.ppermute(partial_other, "vox", SWAP)
    theirs = partial_other + lax.ppermute(partial_own, "vox", SWAP)
    low = jnp.where(core == 0, mine, theirs).reshape(everyone, 1, share, columns)
    high = jnp.where(core == 0, theirs, mine).reshape(everyone, 1, share, columns)
    chip_sum = jnp.concatenate([low, high], axis=1)
    chip_sum, innov_own, innov_other = lax.optimization_barrier((chip_sum, innov_own, innov_other))
    predicted = chip_sum + lax.ppermute(chip_sum, "vox", [(0, 2), (2, 0), (1, 3), (3, 1)])
    minus = minus_inverse(core_array, innov_own, innov_other)
    solved = solve_turned(minus, predicted)

    at_x = device % 4
    at_y = device // 8
    from_x = [lax.ppermute(solved, "obs", steps_along(2, d)) for d in (1, 3, 2)]
    from_y = [lax.ppermute(solved, "obs", steps_along(0, d)) for d in (1, 3, 2)]
    solved, from_x, from_y = lax.optimization_barrier((solved, from_x, from_y))
    parts_x = products([solved] + from_x, cross, 0)
    back_x = [lax.ppermute(part, "obs", steps_along(2, -d)) for part, d in zip(parts_x[1:], (1, 3, 2))]
    parts_y = products([solved] + from_y, cross, 1)
    back_y = [lax.ppermute(part, "obs", steps_along(0, -d)) for part, d in zip(parts_y[1:], (1, 3, 2))]
    chunks = jnp.stack([(at_x + d) % 4 for d in (0, 1, 3, 2)] + [4 + (at_y + d) % 4 for d in (0, 1, 3, 2)])
    parts = [parts_x[0]] + back_x + [parts_y[0]] + back_y
    return downdate(chunks.astype(jnp.int32), parts, cov_slab)


def solution(mesh):
    placed = (
        P("vox", "obs"),
        P("vox", "obs"),
        P("obs", None),
        P("obs", None),
        P("obs"),
        P("obs", None),
    )
    return jax.shard_map(
        shards, mesh=mesh, in_specs=placed, out_specs=P("vox", "obs"), check_vma=False
    )
```

```python
import functools
import math

import jax
import jax.numpy as jnp
from jax import lax
from jax.experimental import pallas as pl
from jax.experimental.pallas import tpu as pltpu
from jax.sharding import PartitionSpec as P

F32 = jnp.float32
BF16 = jnp.bfloat16
VMEM_LIMIT = 60 * 1024 * 1024


def halves(x):
    high = x.astype(BF16)
    return high, (x - high.astype(F32)).astype(BF16)


def dot(a, b):
    return jnp.dot(a, b, preferred_element_type=F32)


def dot_split(a, b):
    ah, al = halves(a)
    bh, bl = halves(b)
    return dot(ah, bh) + (dot(ah, bl) + dot(al, bh))


def split_kernel(cov_ref, out_ref):
    columns = cov_ref.shape[1]
    high, low = halves(cov_ref[...])
    out_ref[:, :columns] = high
    out_ref[:, columns:] = low


def split_slab(cov_slab):
    rows, columns = cov_slab.shape
    tile = 2048
    return pl.pallas_call(
        split_kernel,
        grid=(rows // tile,),
        in_specs=[pl.BlockSpec((tile, columns), lambda i: (i, 0))],
        out_specs=pl.BlockSpec((tile, 2 * columns), lambda i: (i, 0)),
        out_shape=jax.ShapeDtypeStruct((rows, 2 * columns), BF16),
        compiler_params=pltpu.CompilerParams(vmem_limit_bytes=VMEM_LIMIT),
        cost_estimate=pl.CostEstimate(flops=4 * rows * columns, bytes_accessed=8 * rows * columns, transcendentals=0),
        name="split",
    )(cov_slab)


def predict_kernel(place_ref, slots_ref, split_ref, out_ref, dense, *, tile, crossing, block, skip):
    step = pl.program_id(0)
    rows, columns = split_ref.shape
    columns = columns // 2
    pairs = rows // (2 * block)
    deep = 2 * 2 * block
    quads = rows // deep
    lane = lax.broadcasted_iota(jnp.int32, (8, 2 * block), 1)
    sub = lax.broadcasted_iota(jnp.int32, (8, 2 * block), 0)
    upper = (lane >= block).astype(jnp.int32)

    @pl.when(step == 0)
    def _():
        def clear(i, c):
            dense[i] = jnp.zeros_like(dense[i])
            return c

        lax.fori_loop(0, pairs, clear, 0)

    def scatter(group, c):
        row = pl.multiple_of(group * 8, 8)
        first = (step * tile + row) * crossing
        blocks = slots_ref[pl.ds(row, 8), skip + crossing * block :].astype(jnp.int32) & 1
        for n in range(crossing):
            if n % 2 == 0:
                plain = slots_ref[pl.ds(row, 8), pl.ds(skip + n * block, 2 * block)]
                turned = pltpu.roll(plain, block, 1)
                both = jnp.where(upper == 0, plain, turned)
            else:
                both = jnp.where(upper == 0, turned, plain)
            half = blocks[:, n : n + 1] == upper
            for i in range(8):
                where = place_ref[first + i * crossing + n]
                pltpu.store(dense.at[where, pl.ds(row, 8), :], both, mask=half & (sub == i))
        return c

    lax.fori_loop(0, tile // 8, scatter, 0)
    out_ref[...] = jnp.zeros_like(out_ref)
    together = 8

    def multiply(i, c):
        wide_sum = jnp.zeros((tile, 2 * columns), F32)
        small = jnp.zeros((tile, columns), F32)
        for k in range(together):
            q = i * together + k
            here = pl.ds(pl.multiple_of(q * deep, deep), deep)
            wide = jnp.concatenate([dense[2 * q], dense[2 * q + 1]], axis=1)
            high, low = halves(wide)
            wide_sum = wide_sum + dot(high, split_ref[here, :])
            small = small + dot(low, split_ref[here, :columns])
            dense[2 * q] = jnp.zeros((tile, 2 * block), F32)
            dense[2 * q + 1] = jnp.zeros((tile, 2 * block), F32)
        out_ref[...] += wide_sum[:, :columns] + (wide_sum[:, columns:] + small)
        return c

    lax.fori_loop(0, quads // together, multiply, 0)


def predict(slots, skip, slab_split, first_block, local_blocks, crossing, block):
    count, width = slots.shape
    rows, columns = slab_split.shape
    columns = columns // 2
    tile = 256
    lanes = skip + crossing * block
    blocks = slots[:, lanes : lanes + crossing].astype(jnp.int32)
    local = blocks - first_block
    inside = (local >= 0) & (local < local_blocks) & (blocks >= 0)
    place = jnp.where(inside, local // 2, local_blocks // 2).reshape(-1)
    return pl.pallas_call(
        functools.partial(predict_kernel, tile=tile, crossing=crossing, block=block, skip=skip),
        grid_spec=pltpu.PrefetchScalarGridSpec(
            num_scalar_prefetch=1,
            grid=(count // tile,),
            in_specs=[
                pl.BlockSpec((tile, width), lambda i, place: (i, 0)),
                pl.BlockSpec(memory_space=pltpu.VMEM),
            ],
            out_specs=pl.BlockSpec((tile, columns), lambda i, place: (i, 0)),
            scratch_shapes=[pltpu.VMEM((rows // (2 * block) + 1, tile, 2 * block), F32)],
        ),
        out_shape=jax.ShapeDtypeStruct((count, columns), F32),
        compiler_params=pltpu.CompilerParams(vmem_limit_bytes=VMEM_LIMIT),
        cost_estimate=pl.CostEstimate(
            flops=12 * count * rows * columns, bytes_accessed=rows * columns * 4, transcendentals=0
        ),
        name="predict",
    )(place, slots, slab_split)


def sweep_rows(rows, first):
    sub = lax.broadcasted_iota(jnp.int32, rows.shape, 0)
    lane = lax.broadcasted_iota(jnp.int32, rows.shape, 1) - first
    cols = [jnp.broadcast_to(rows[:, first + j : first + j + 1], rows.shape) for j in range(8)]

    def row(v, p):
        return jnp.broadcast_to(v[p : p + 1, :], rows.shape)

    out = rows
    for p in range(0, 8, 2):
        q = p + 1
        a, b, d = row(cols[p], p), row(cols[q], p), row(cols[q], q)
        inv = 1.0 / (a * d - b * b)
        a, b, d = a * inv, b * inv, d * inv
        out = jnp.where((lane == p) | (lane == q), jnp.where(sub == lane, 1.0, 0.0), out)

        def eliminate(v):
            at_p, at_q = row(v, p), row(v, q)
            new_p = d * at_p - b * at_q
            new_q = a * at_q - b * at_p
            rest = v - cols[p] * new_p - cols[q] * new_q
            return jnp.where(sub == p, new_p, jnp.where(sub == q, new_q, rest))

        out = eliminate(out)
        cols = [eliminate(col) if j > q else col for j, col in enumerate(cols)]
    return jnp.where((lane >= 0) & (lane < 8), -out, out)


def small_sweep(block):
    size = block.shape[0]
    strip = 16
    lanes = lax.broadcasted_iota(jnp.int32, (8, size), 1)
    all_lanes = lax.broadcasted_iota(jnp.int32, (size, size), 1)
    for base in range(0, size, strip):
        rows = [block[at : at + 8, :] for at in range(base, base + strip, 8)]
        for g in range(strip // 8):
            first = base + 8 * g
            top = sweep_rows(rows[g], first)
            pivots = (lanes >= first) & (lanes < first + 8)
            for e in range(strip // 8):
                if e != g:
                    rest = jnp.where(pivots, 0.0, rows[e])
                    for j in range(8):
                        rest = rest - rows[e][:, first + j : first + j + 1] * top[j : j + 1, :]
                    rows[e] = rest
            rows[g] = top
        middle = jnp.concatenate(rows, axis=0)
        above = [jnp.zeros((base, size), F32)] if base else []
        below = [jnp.zeros((size - base - strip, size), F32)] if base + strip < size else []
        high, low = halves(jnp.concatenate(above + [middle] + below, axis=0))
        block_high, block_low = halves(block)
        keep = jnp.where((all_lanes >= base) & (all_lanes < base + strip), 0.0, block)
        new = keep - (
            dot(jnp.concatenate([block_high, block_low], axis=1), jnp.concatenate([high, high], axis=0))
            + dot(block_high, low)
        )
        above = [new[:base]] if base else []
        below = [new[base + strip :]] if base + strip < size else []
        block = jnp.concatenate(above + [middle] + below, axis=0)
    return block


def inverse_kernel(core_ref, own_ref, other_ref, m_ref, left, right, pivot, *, size):
    n = m_ref.shape[0]
    regions, share, lanes = own_ref.shape
    core = core_ref[0]
    blocks = n // size
    per_block = regions // blocks

    def place(i, c):
        mine = pl.multiple_of((2 * i + core) * share, share)
        theirs = pl.multiple_of((2 * i + 1 - core) * share, share)
        for j in range(lanes // size):
            at = pl.ds(pl.multiple_of(lax.rem(lax.div(i, per_block) + j, blocks) * size, size), size)
            m_ref[pl.ds(mine, share), at] = own_ref[i, :, j * size : (j + 1) * size]
            m_ref[pl.ds(theirs, share), at] = other_ref[i, :, j * size : (j + 1) * size]
        return c

    lax.fori_loop(0, regions, place, 0)

    def mirror(i, c):
        at = pl.ds(pl.multiple_of(i * size, size), size)
        for j in range(1, blocks - lanes // size + 1):
            to = pl.ds(pl.multiple_of(lax.rem(i + j, blocks) * size, size), size)
            m_ref[to, at] = m_ref[at, to].T
        return c

    lax.fori_loop(0, blocks, mirror, 0)

    def sweep(k, c):
        at = pl.ds(pl.multiple_of(k * size, size), size)
        minus = small_sweep(m_ref[at, at])
        pivot[...] = dot_split(minus, m_ref[at, :]) * -1.0
        pivot[:, at] = minus
        high, low = halves(m_ref[:, at])
        left[:, :size] = high
        left[:, size:] = low
        m_ref[:, at] = jnp.zeros((n, size), F32)
        high, low = halves(pivot[...])
        right[:size, :] = high
        right[size : 2 * size, :] = high
        right[2 * size :, :] = low
        wide = n // 2

        def update(i, c):
            here = pl.ds(pl.multiple_of(i * wide, wide), wide)
            product = dot(left[...], right[: 2 * size, here]) + dot(left[:, :size], right[2 * size :, here])
            m_ref[:, here] = m_ref[:, here] - product
            return c

        lax.fori_loop(0, n // wide, update, 0)
        m_ref[at, :] = pivot[...]
        return c

    lax.fori_loop(0, n // size, sweep, 0)


def minus_inverse(core, own, other, lanes):
    regions, share, _ = own.shape
    n = 2 * regions * share
    size = 128
    return pl.pallas_call(
        functools.partial(inverse_kernel, size=size),
        grid=(1,),
        in_specs=[pl.BlockSpec(memory_space=pltpu.SMEM)]
        + [pl.BlockSpec((regions, share, lanes), lambda i: (0, 0, 0))] * 2,
        out_specs=pl.BlockSpec(memory_space=pltpu.VMEM),
        out_shape=jax.ShapeDtypeStruct((n, n), F32),
        scratch_shapes=[
            pltpu.VMEM((n, 2 * size), BF16),
            pltpu.VMEM((3 * size, n), BF16),
            pltpu.VMEM((size, n), F32),
        ],
        compiler_params=pltpu.CompilerParams(vmem_limit_bytes=VMEM_LIMIT),
        cost_estimate=pl.CostEstimate(flops=60 * n * n * n, bytes_accessed=8 * n * n, transcendentals=0),
        name="minus_inverse",
    )(core, own, other)


def solve_kernel(minus_ref, predicted_ref, out_ref):
    predicted = predicted_ref[...].reshape(minus_ref.shape[0], -1)
    out_ref[...] = (-dot_split(predicted.T, minus_ref[...])).astype(BF16)


def solve_turned(minus, predicted):
    n, columns = minus.shape[0], predicted.shape[-1]
    return pl.pallas_call(
        solve_kernel,
        in_specs=[pl.BlockSpec(memory_space=pltpu.VMEM)] * 2,
        out_specs=pl.BlockSpec(memory_space=pltpu.VMEM),
        out_shape=jax.ShapeDtypeStruct((columns, n), BF16),
        compiler_params=pltpu.CompilerParams(vmem_limit_bytes=VMEM_LIMIT),
        cost_estimate=pl.CostEstimate(flops=6 * n * n * columns, bytes_accessed=4 * n * n, transcendentals=0),
        name="solve",
    )(minus, predicted)


def spread_kernel(by_x_ref, by_y_ref, out_ref):
    out_ref[0, 0] = by_x_ref[...]
    out_ref[0, 1] = by_y_ref[...]


def spread(turned):
    slots, rows = turned.shape
    width = rows // 8
    everyone = math.prod(SIZES)
    return pl.pallas_call(
        spread_kernel,
        grid=(everyone,),
        in_specs=[
            pl.BlockSpec((slots, width), lambda i: (0, i % 4)),
            pl.BlockSpec((slots, width), lambda i: (0, 4 + i // 8)),
        ],
        out_specs=pl.BlockSpec((1, 2, slots, width), lambda i: (i, 0, 0, 0)),
        out_shape=jax.ShapeDtypeStruct((everyone, 2, slots, width), turned.dtype),
        compiler_params=pltpu.CompilerParams(vmem_limit_bytes=VMEM_LIMIT),
        cost_estimate=pl.CostEstimate(flops=0, bytes_accessed=16 * slots * rows, transcendentals=0),
        name="spread",
    )(turned, turned)


def product_kernel(*refs, members):
    solved_refs, cross_ref, out_refs, stack = refs[:members], refs[members], refs[members + 1 : -1], refs[-1]
    columns = solved_refs[0].shape[0]

    @pl.when(pl.program_id(0) == 0)
    def _():
        for i, ref in enumerate(solved_refs):
            stack[i * columns : (i + 1) * columns, :] = ref[...]

    everyone, _, slots, tile = cross_ref.shape
    product = dot(stack[...], cross_ref[...].reshape(everyone * slots, tile))
    for i, ref in enumerate(out_refs):
        ref[...] = product[i * columns : (i + 1) * columns, :].astype(ref.dtype)


def products(solved, cross, half):
    members = len(solved)
    columns, n = solved[0].shape
    everyone, _, slots, width = cross.shape
    tile = 512
    return pl.pallas_call(
        functools.partial(product_kernel, members=members),
        grid=(width // tile,),
        in_specs=[pl.BlockSpec(memory_space=pltpu.VMEM)] * members
        + [pl.BlockSpec((everyone, 1, slots, tile), lambda i: (0, half, 0, i))],
        out_specs=[pl.BlockSpec((columns, tile), lambda i: (0, i))] * members,
        out_shape=[jax.ShapeDtypeStruct((columns, width), BF16 if i else F32) for i in range(members)],
        scratch_shapes=[pltpu.VMEM((members * columns, n), BF16)],
        compiler_params=pltpu.CompilerParams(vmem_limit_bytes=VMEM_LIMIT),
        cost_estimate=pl.CostEstimate(
            flops=2 * members * columns * n * width, bytes_accessed=2 * n * width, transcendentals=0
        ),
        name="products",
    )(*solved, cross)


def downdate_kernel(chunk_ref, *refs, pieces):
    product_refs, cov_ref, out_ref = refs[:-2], refs[-2], refs[-1]
    tile = cov_ref.shape[0]
    for i, ref in enumerate(product_refs):
        for k in range(pieces):

            @pl.when(pl.program_id(0) == i * pieces + k)
            def _():
                out_ref[...] = cov_ref[...] - ref[:, k * tile : (k + 1) * tile].T.astype(F32)


def downdate(chunks, parts, cov_slab):
    rows, columns = cov_slab.shape
    pieces = 1
    tile = rows // (len(parts) * pieces)
    spec = pl.BlockSpec((tile, columns), lambda i, chunk: (chunk[i // pieces] * pieces + i % pieces, 0))
    return pl.pallas_call(
        functools.partial(downdate_kernel, pieces=pieces),
        grid_spec=pltpu.PrefetchScalarGridSpec(
            num_scalar_prefetch=1,
            grid=(len(parts) * pieces,),
            in_specs=[pl.BlockSpec(memory_space=pltpu.VMEM)] * len(parts) + [spec],
            out_specs=spec,
        ),
        out_shape=jax.ShapeDtypeStruct((rows, columns), F32),
        compiler_params=pltpu.CompilerParams(vmem_limit_bytes=VMEM_LIMIT),
        cost_estimate=pl.CostEstimate(flops=rows * columns, bytes_accessed=10 * rows * columns, transcendentals=0),
        name="downdate",
    )(chunks, *parts, cov_slab)


def merged(ray_blocks, weights):
    slots, crossing = ray_blocks.shape
    same = ray_blocks[:, :, None] == ray_blocks[:, None, :]
    order = jnp.arange(crossing, dtype=jnp.int32)
    first = ~jnp.any(same & (order[None, None, :] < order[None, :, None]), axis=2)
    parts = weights.reshape(slots, crossing, -1)
    total = jnp.sum(jnp.where(same[:, :, :, None], parts[:, None, :, :], 0.0), axis=2)
    return jnp.where(first, ray_blocks, -1), total.reshape(weights.shape)


SIZES = (4, 2, 4)
SWAP = [(0, 1), (1, 0), (2, 3), (3, 2)]


def steps_along(axis, distance):
    pairs = []
    for y in range(SIZES[0]):
        for z in range(SIZES[1]):
            for x in range(SIZES[2]):
                to = [y, z, x]
                to[axis] = (to[axis] + distance) % SIZES[axis]
                pairs.append(((y * SIZES[1] + z) * SIZES[2] + x, (to[0] * SIZES[1] + to[1]) * SIZES[2] + to[2]))
    return pairs


def to_all(piece):
    everyone = math.prod(SIZES)
    return lax.all_to_all(jnp.broadcast_to(piece[None], (everyone,) + piece.shape), "obs", 0, 0)


def shards(cov_slab, cross_cov, ray_blocks, ray_coeff, region_rows, innov_cov):
    local_rows, columns = cov_slab.shape
    slot_count, crossing = ray_blocks.shape
    block_size = ray_coeff.shape[1] // crossing
    local_blocks = local_rows // block_size
    everyone = math.prod(SIZES)
    device = lax.axis_index("obs")
    core = lax.axis_index("vox") % 2
    core_array = core.astype(jnp.int32).reshape(1)
    share = slot_count // 2
    start = core * share

    my_blocks = lax.dynamic_slice_in_dim(ray_blocks, start, share, 0)
    my_coeff = lax.dynamic_slice_in_dim(ray_coeff, start, share, 0)
    live = start + jnp.arange(share, dtype=jnp.int32) < region_rows[0]
    weights = jnp.where(live[:, None], my_coeff, 0.0)
    blocks, weights = merged(my_blocks, weights)
    my_innov = lax.dynamic_slice_in_dim(innov_cov, start, share, 0)
    skip = 640
    my_innov = lax.dynamic_slice_in_dim(jnp.concatenate([my_innov, my_innov], axis=1), device // 4 * 128, skip, 1)
    message = jnp.concatenate([my_innov, weights, jnp.pad(blocks.astype(F32), ((0, 0), (0, 128 - crossing)))], axis=1)
    own = to_all(message)

    slab_split = split_slab(cov_slab)
    send = spread(cross_cov.T)
    own, send, slab_split = lax.optimization_barrier((own, send, slab_split))
    cross = lax.all_to_all(send, "obs", 0, 0)
    other = lax.ppermute(own, "vox", SWAP)
    first_block = lax.axis_index("vox") * local_blocks
    flat = (everyone * share, -1)
    partial_own = predict(own.reshape(flat), skip, slab_split, first_block, local_blocks, crossing, block_size)
    other, partial_own = lax.optimization_barrier((other, partial_own))
    partial_other = predict(other.reshape(flat), skip, slab_split, first_block, local_blocks, crossing, block_size)

    mine = partial_own + lax.ppermute(partial_other, "vox", SWAP)
    theirs = partial_other + lax.ppermute(partial_own, "vox", SWAP)
    low = jnp.where(core == 0, mine, theirs).reshape(everyone, 1, share, columns)
    high = jnp.where(core == 0, theirs, mine).reshape(everyone, 1, share, columns)
    chip_sum = jnp.concatenate([low, high], axis=1)
    chip_sum, other = lax.optimization_barrier((chip_sum, other))
    predicted = chip_sum + lax.ppermute(chip_sum, "vox", [(0, 2), (2, 0), (1, 3), (3, 1)])
    minus = minus_inverse(core_array, own, other, skip)
    solved = solve_turned(minus, predicted)

    at_x = device % 4
    at_y = device // 8
    from_x = [lax.ppermute(solved, "obs", steps_along(2, d)) for d in (1, 3, 2)]
    from_y = [lax.ppermute(solved, "obs", steps_along(0, d)) for d in (1, 3, 2)]
    solved, from_x, from_y = lax.optimization_barrier((solved, from_x, from_y))
    parts_x = products([solved] + from_x, cross, 0)
    back_x = [lax.ppermute(part, "obs", steps_along(2, -d)) for part, d in zip(parts_x[1:], (1, 3, 2))]
    parts_y = products([solved] + from_y, cross, 1)
    back_y = [lax.ppermute(part, "obs", steps_along(0, -d)) for part, d in zip(parts_y[1:], (1, 3, 2))]
    chunks = jnp.stack([(at_x + d) % 4 for d in (0, 1, 3, 2)] + [4 + (at_y + d) % 4 for d in (0, 1, 3, 2)])
    parts = [parts_x[0]] + back_x + [parts_y[0]] + back_y
    return downdate(chunks.astype(jnp.int32), parts, cov_slab)


def solution(mesh):
    placed = (
        P("vox", "obs"),
        P("vox", "obs"),
        P("obs", None),
        P("obs", None),
        P("obs"),
        P("obs", None),
    )
    return jax.shard_map(
        shards, mesh=mesh, in_specs=placed, out_specs=P("vox", "obs"), check_vma=False
    )
```

```python
import functools
import math

import jax
import jax.numpy as jnp
from jax import lax
from jax.experimental import pallas as pl
from jax.experimental.pallas import tpu as pltpu
from jax.sharding import PartitionSpec as P

F32 = jnp.float32
BF16 = jnp.bfloat16
VMEM_LIMIT = 60 * 1024 * 1024


def halves(x):
    high = x.astype(BF16)
    return high, (x - high.astype(F32)).astype(BF16)


def dot(a, b):
    return jnp.dot(a, b, preferred_element_type=F32)


def dot_split(a, b):
    ah, al = halves(a)
    bh, bl = halves(b)
    return dot(ah, bh) + (dot(ah, bl) + dot(al, bh))


def split_kernel(cov_ref, out_ref):
    columns = cov_ref.shape[1]
    high, low = halves(cov_ref[...])
    out_ref[:, :columns] = high
    out_ref[:, columns:] = low


def split_slab(cov_slab):
    rows, columns = cov_slab.shape
    tile = 2048
    return pl.pallas_call(
        split_kernel,
        grid=(rows // tile,),
        in_specs=[pl.BlockSpec((tile, columns), lambda i: (i, 0))],
        out_specs=pl.BlockSpec((tile, 2 * columns), lambda i: (i, 0)),
        out_shape=jax.ShapeDtypeStruct((rows, 2 * columns), BF16),
        compiler_params=pltpu.CompilerParams(vmem_limit_bytes=VMEM_LIMIT),
        cost_estimate=pl.CostEstimate(flops=4 * rows * columns, bytes_accessed=8 * rows * columns, transcendentals=0),
        name="split",
    )(cov_slab)


def predict_kernel(place_ref, slots_ref, far_ref, out_ref, dense, split_ref, arrived, *, tile, crossing, block, skip):
    step = pl.program_id(0)
    fetch = pltpu.make_async_copy(far_ref, split_ref, arrived)
    rows, columns = split_ref.shape
    columns = columns // 2
    pairs = rows // (2 * block)
    deep = 2 * 2 * block
    quads = rows // deep
    lane = lax.broadcasted_iota(jnp.int32, (8, 2 * block), 1)
    sub = lax.broadcasted_iota(jnp.int32, (8, 2 * block), 0)
    upper = (lane >= block).astype(jnp.int32)

    @pl.when(step == 0)
    def _():
        fetch.start()

        def clear(i, c):
            dense[i] = jnp.zeros_like(dense[i])
            return c

        lax.fori_loop(0, pairs, clear, 0)

    def scatter(group, c):
        row = pl.multiple_of(group * 8, 8)
        first = (step * tile + row) * crossing
        blocks = slots_ref[pl.ds(row, 8), skip + crossing * block :].astype(jnp.int32) & 1
        for n in range(crossing):
            if n % 2 == 0:
                plain = slots_ref[pl.ds(row, 8), pl.ds(skip + n * block, 2 * block)]
                turned = pltpu.roll(plain, block, 1)
                both = jnp.where(upper == 0, plain, turned)
            else:
                both = jnp.where(upper == 0, turned, plain)
            half = blocks[:, n : n + 1] == upper
            for i in range(8):
                where = place_ref[first + i * crossing + n]
                pltpu.store(dense.at[where, pl.ds(row, 8), :], both, mask=half & (sub == i))
        return c

    lax.fori_loop(0, tile // 8, scatter, 0)
    out_ref[...] = jnp.zeros_like(out_ref)
    together = 16

    @pl.when(step == 0)
    def _():
        fetch.wait()

    def multiply(i, c):
        wide_sum = jnp.zeros((tile, 2 * columns), F32)
        small = jnp.zeros((tile, columns), F32)
        for k in range(together):
            q = i * together + k
            here = pl.ds(pl.multiple_of(q * deep, deep), deep)
            wide = jnp.concatenate([dense[2 * q], dense[2 * q + 1]], axis=1)
            high, low = halves(wide)
            wide_sum = wide_sum + dot(high, split_ref[here, :])
            small = small + dot(low, split_ref[here, :columns])
            dense[2 * q] = jnp.zeros((tile, 2 * block), F32)
            dense[2 * q + 1] = jnp.zeros((tile, 2 * block), F32)
        out_ref[...] += wide_sum[:, :columns] + (wide_sum[:, columns:] + small)
        return c

    lax.fori_loop(0, quads // together, multiply, 0)


def predict(slots, skip, slab_split, first_block, local_blocks, crossing, block):
    count, width = slots.shape
    rows, columns = slab_split.shape
    columns = columns // 2
    tile = 256
    lanes = skip + crossing * block
    blocks = slots[:, lanes : lanes + crossing].astype(jnp.int32)
    local = blocks - first_block
    inside = (local >= 0) & (local < local_blocks) & (blocks >= 0)
    place = jnp.where(inside, local // 2, local_blocks // 2).reshape(-1)
    return pl.pallas_call(
        functools.partial(predict_kernel, tile=tile, crossing=crossing, block=block, skip=skip),
        grid_spec=pltpu.PrefetchScalarGridSpec(
            num_scalar_prefetch=1,
            grid=(count // tile,),
            in_specs=[
                pl.BlockSpec((tile, width), lambda i, place: (i, 0)),
                pl.BlockSpec(memory_space=pl.ANY),
            ],
            out_specs=pl.BlockSpec((tile, columns), lambda i, place: (i, 0)),
            scratch_shapes=[
                pltpu.VMEM((rows // (2 * block) + 1, tile, 2 * block), F32),
                pltpu.VMEM((rows, 2 * columns), BF16),
                pltpu.SemaphoreType.DMA,
            ],
        ),
        out_shape=jax.ShapeDtypeStruct((count, columns), F32),
        compiler_params=pltpu.CompilerParams(vmem_limit_bytes=VMEM_LIMIT),
        cost_estimate=pl.CostEstimate(
            flops=12 * count * rows * columns, bytes_accessed=rows * columns * 4, transcendentals=0
        ),
        name="predict",
    )(place, slots, slab_split)


def spread_lane(rows, lane):
    return jnp.take_along_axis(rows, jnp.full(rows.shape, lane, jnp.int32), axis=1)


def sweep_rows(rows, first):
    sub = lax.broadcasted_iota(jnp.int32, rows.shape, 0)
    lane = lax.broadcasted_iota(jnp.int32, rows.shape, 1) - first
    cols = [spread_lane(rows, first + j) for j in range(8)]

    def row(v, p):
        return jnp.broadcast_to(v[p : p + 1, :], rows.shape)

    out = rows
    for p in range(0, 8, 2):
        q = p + 1
        a, b, d = row(cols[p], p), row(cols[q], p), row(cols[q], q)
        inv = 1.0 / (a * d - b * b)
        a, b, d = a * inv, b * inv, d * inv
        out = jnp.where((lane == p) | (lane == q), jnp.where(sub == lane, 1.0, 0.0), out)

        def eliminate(v):
            at_p, at_q = row(v, p), row(v, q)
            new_p = d * at_p - b * at_q
            new_q = a * at_q - b * at_p
            rest = v - cols[p] * new_p - cols[q] * new_q
            return jnp.where(sub == p, new_p, jnp.where(sub == q, new_q, rest))

        out = eliminate(out)
        cols = [eliminate(col) if j > q else col for j, col in enumerate(cols)]
    return jnp.where((lane >= 0) & (lane < 8), -out, out)


def take_away(rows, swept, first):
    lanes = lax.broadcasted_iota(jnp.int32, rows.shape, 1)
    count = swept.shape[0]
    even = jnp.where((lanes >= first) & (lanes < first + count), 0.0, rows)
    odd = jnp.zeros_like(rows)
    for j in range(0, count, 2):
        even = even - spread_lane(rows, first + j) * swept[j : j + 1, :]
        odd = odd + spread_lane(rows, first + j + 1) * swept[j + 1 : j + 2, :]
    return even - odd


def small_sweep(block):
    size = block.shape[0]
    strip = 16
    all_lanes = lax.broadcasted_iota(jnp.int32, (size, size), 1)
    rows = [block[at : at + 8, :] for at in range(0, strip, 8)]
    for base in range(0, size, strip):
        for g in range(strip // 8):
            top = sweep_rows(rows[g], base + 8 * g)
            rows = [top if e == g else take_away(rows[e], top, base + 8 * g) for e in range(strip // 8)]
        middle = jnp.concatenate(rows, axis=0)
        after = base + strip
        ahead = [take_away(block[at : at + 8, :], middle, base) for at in range(after, min(after + strip, size), 8)]
        above = [jnp.zeros((base, size), F32)] if base else []
        below = [jnp.zeros((size - after, size), F32)] if after < size else []
        high, low = halves(jnp.concatenate(above + [middle] + below, axis=0))
        block_high, block_low = halves(block)
        keep = jnp.where((all_lanes >= base) & (all_lanes < after), 0.0, block)
        new = keep - (
            dot(jnp.concatenate([block_high, block_low], axis=1), jnp.concatenate([high, high], axis=0))
            + dot(block_high, low)
        )
        above = [new[:base]] if base else []
        below = [new[after + strip :]] if after + strip < size else []
        block = jnp.concatenate(above + [middle] + ahead + below, axis=0)
        rows = ahead
    return block


def inverse_kernel(core_ref, own_ref, other_ref, m_ref, left, right, pivot, *, size):
    n = m_ref.shape[0]
    regions, share, lanes = own_ref.shape
    core = core_ref[0]
    blocks = n // size
    per_block = regions // blocks

    def place(i, c):
        mine = pl.multiple_of((2 * i + core) * share, share)
        theirs = pl.multiple_of((2 * i + 1 - core) * share, share)
        for j in range(lanes // size):
            at = pl.ds(pl.multiple_of(lax.rem(lax.div(i, per_block) + j, blocks) * size, size), size)
            m_ref[pl.ds(mine, share), at] = own_ref[i, :, j * size : (j + 1) * size]
            m_ref[pl.ds(theirs, share), at] = other_ref[i, :, j * size : (j + 1) * size]
        return c

    lax.fori_loop(0, regions, place, 0)

    def mirror(i, c):
        at = pl.ds(pl.multiple_of(i * size, size), size)
        for j in range(1, blocks - lanes // size + 1):
            to = pl.ds(pl.multiple_of(lax.rem(i + j, blocks) * size, size), size)
            m_ref[to, at] = m_ref[at, to].T
        return c

    lax.fori_loop(0, blocks, mirror, 0)

    def sweep(k, c):
        at = pl.ds(pl.multiple_of(k * size, size), size)
        minus = small_sweep(m_ref[at, at])
        pivot[...] = dot_split(minus, m_ref[at, :]) * -1.0
        pivot[:, at] = minus
        high, low = halves(m_ref[:, at])
        left[:, :size] = high
        left[:, size:] = low
        m_ref[:, at] = jnp.zeros((n, size), F32)
        high, low = halves(pivot[...])
        right[:size, :] = high
        right[size : 2 * size, :] = high
        right[2 * size :, :] = low
        product = dot(left[...], right[: 2 * size, :]) + dot(left[:, :size], right[2 * size :, :])
        m_ref[...] = m_ref[...] - product
        m_ref[at, :] = pivot[...]
        return c

    lax.fori_loop(0, n // size, sweep, 0)


def minus_inverse(core, own, other, lanes):
    regions, share, _ = own.shape
    n = 2 * regions * share
    size = 128
    return pl.pallas_call(
        functools.partial(inverse_kernel, size=size),
        grid=(1,),
        in_specs=[pl.BlockSpec(memory_space=pltpu.SMEM)]
        + [pl.BlockSpec((regions, share, lanes), lambda i: (0, 0, 0))] * 2,
        out_specs=pl.BlockSpec(memory_space=pltpu.VMEM),
        out_shape=jax.ShapeDtypeStruct((n, n), F32),
        scratch_shapes=[
            pltpu.VMEM((n, 2 * size), BF16),
            pltpu.VMEM((3 * size, n), BF16),
            pltpu.VMEM((size, n), F32),
        ],
        compiler_params=pltpu.CompilerParams(vmem_limit_bytes=VMEM_LIMIT),
        cost_estimate=pl.CostEstimate(flops=60 * n * n * n, bytes_accessed=8 * n * n, transcendentals=0),
        name="minus_inverse",
    )(core, own, other)


def solve_kernel(minus_ref, predicted_ref, out_ref):
    predicted = predicted_ref[...].reshape(minus_ref.shape[0], -1)
    out_ref[...] = (-dot_split(predicted.T, minus_ref[...])).astype(BF16)


def solve_turned(minus, predicted):
    n, columns = minus.shape[0], predicted.shape[-1]
    return pl.pallas_call(
        solve_kernel,
        in_specs=[pl.BlockSpec(memory_space=pltpu.VMEM)] * 2,
        out_specs=pl.BlockSpec(memory_space=pltpu.VMEM),
        out_shape=jax.ShapeDtypeStruct((columns, n), BF16),
        compiler_params=pltpu.CompilerParams(vmem_limit_bytes=VMEM_LIMIT),
        cost_estimate=pl.CostEstimate(flops=6 * n * n * columns, bytes_accessed=4 * n * n, transcendentals=0),
        name="solve",
    )(minus, predicted)


def spread_kernel(by_x_ref, by_y_ref, out_ref):
    out_ref[0, 0] = by_x_ref[...]
    out_ref[0, 1] = by_y_ref[...]


def spread(turned):
    slots, rows = turned.shape
    width = rows // 8
    everyone = math.prod(SIZES)
    return pl.pallas_call(
        spread_kernel,
        grid=(everyone,),
        in_specs=[
            pl.BlockSpec((slots, width), lambda i: (0, i % 4)),
            pl.BlockSpec((slots, width), lambda i: (0, 4 + i // 8)),
        ],
        out_specs=pl.BlockSpec((1, 2, slots, width), lambda i: (i, 0, 0, 0)),
        out_shape=jax.ShapeDtypeStruct((everyone, 2, slots, width), turned.dtype),
        compiler_params=pltpu.CompilerParams(vmem_limit_bytes=VMEM_LIMIT),
        cost_estimate=pl.CostEstimate(flops=0, bytes_accessed=16 * slots * rows, transcendentals=0),
        name="spread",
    )(turned, turned)


def product_kernel(*refs, members):
    solved_refs, cross_ref, out_refs, stack = refs[:members], refs[members], refs[members + 1 : -1], refs[-1]
    columns = solved_refs[0].shape[0]

    @pl.when(pl.program_id(0) == 0)
    def _():
        for i, ref in enumerate(solved_refs):
            stack[i * columns : (i + 1) * columns, :] = ref[...]

    everyone, _, slots, tile = cross_ref.shape
    product = dot(stack[...], cross_ref[...].reshape(everyone * slots, tile))
    for i, ref in enumerate(out_refs):
        ref[...] = product[i * columns : (i + 1) * columns, :].astype(ref.dtype)


def products(solved, cross, half):
    members = len(solved)
    columns, n = solved[0].shape
    everyone, _, slots, width = cross.shape
    tile = 512
    return pl.pallas_call(
        functools.partial(product_kernel, members=members),
        grid=(width // tile,),
        in_specs=[pl.BlockSpec(memory_space=pltpu.VMEM)] * members
        + [pl.BlockSpec((everyone, 1, slots, tile), lambda i: (0, half, 0, i))],
        out_specs=[pl.BlockSpec((columns, tile), lambda i: (0, i))] * members,
        out_shape=[jax.ShapeDtypeStruct((columns, width), BF16 if i else F32) for i in range(members)],
        scratch_shapes=[pltpu.VMEM((members * columns, n), BF16)],
        compiler_params=pltpu.CompilerParams(vmem_limit_bytes=VMEM_LIMIT),
        cost_estimate=pl.CostEstimate(
            flops=2 * members * columns * n * width, bytes_accessed=2 * n * width, transcendentals=0
        ),
        name="products",
    )(*solved, cross)


def downdate_kernel(chunk_ref, *refs, count):
    product_refs, cov_ref, out_ref = refs[:count], refs[count], refs[-1]
    for i, ref in enumerate(product_refs):

        @pl.when(pl.program_id(0) == i)
        def _():
            out_ref[...] = cov_ref[...] - ref[...].T.astype(F32)


def downdate(chunks, parts, cov_slab, so_far=None):
    rows, columns = cov_slab.shape
    count = len(parts)
    tile = parts[0].shape[1]
    spec = pl.BlockSpec((tile, columns), lambda i, chunk: (chunk[i], 0))
    more = [] if so_far is None else [so_far]
    return pl.pallas_call(
        functools.partial(downdate_kernel, count=count),
        grid_spec=pltpu.PrefetchScalarGridSpec(
            num_scalar_prefetch=1,
            grid=(count,),
            in_specs=[pl.BlockSpec(memory_space=pltpu.VMEM)] * count
            + [spec]
            + [pl.BlockSpec(memory_space=pl.ANY)] * len(more),
            out_specs=spec,
        ),
        out_shape=jax.ShapeDtypeStruct((rows, columns), F32),
        input_output_aliases={count + 2: 0} if more else {},
        compiler_params=pltpu.CompilerParams(vmem_limit_bytes=VMEM_LIMIT),
        cost_estimate=pl.CostEstimate(
            flops=count * tile * columns, bytes_accessed=10 * count * tile * columns, transcendentals=0
        ),
        name="downdate",
    )(jnp.stack(chunks).astype(jnp.int32), *parts, cov_slab, *more)


def merged(ray_blocks, weights):
    slots, crossing = ray_blocks.shape
    same = ray_blocks[:, :, None] == ray_blocks[:, None, :]
    order = jnp.arange(crossing, dtype=jnp.int32)
    first = ~jnp.any(same & (order[None, None, :] < order[None, :, None]), axis=2)
    parts = weights.reshape(slots, crossing, -1)
    total = jnp.sum(jnp.where(same[:, :, :, None], parts[:, None, :, :], 0.0), axis=2)
    return jnp.where(first, ray_blocks, -1), total.reshape(weights.shape)


SIZES = (4, 2, 4)
SWAP = [(0, 1), (1, 0), (2, 3), (3, 2)]


def steps_along(axis, distance):
    pairs = []
    for y in range(SIZES[0]):
        for z in range(SIZES[1]):
            for x in range(SIZES[2]):
                to = [y, z, x]
                to[axis] = (to[axis] + distance) % SIZES[axis]
                pairs.append(((y * SIZES[1] + z) * SIZES[2] + x, (to[0] * SIZES[1] + to[1]) * SIZES[2] + to[2]))
    return pairs


def to_all(piece):
    everyone = math.prod(SIZES)
    return lax.all_to_all(jnp.broadcast_to(piece[None], (everyone,) + piece.shape), "obs", 0, 0)


def shards(cov_slab, cross_cov, ray_blocks, ray_coeff, region_rows, innov_cov):
    local_rows, columns = cov_slab.shape
    slot_count, crossing = ray_blocks.shape
    block_size = ray_coeff.shape[1] // crossing
    local_blocks = local_rows // block_size
    everyone = math.prod(SIZES)
    device = lax.axis_index("obs")
    core = lax.axis_index("vox") % 2
    core_array = core.astype(jnp.int32).reshape(1)
    share = slot_count // 2
    start = core * share

    my_blocks = lax.dynamic_slice_in_dim(ray_blocks, start, share, 0)
    my_coeff = lax.dynamic_slice_in_dim(ray_coeff, start, share, 0)
    live = start + jnp.arange(share, dtype=jnp.int32) < region_rows[0]
    weights = jnp.where(live[:, None], my_coeff, 0.0)
    blocks, weights = merged(my_blocks, weights)
    my_innov = lax.dynamic_slice_in_dim(innov_cov, start, share, 0)
    skip = 640
    my_innov = lax.dynamic_slice_in_dim(jnp.concatenate([my_innov, my_innov], axis=1), device // 4 * 128, skip, 1)
    message = jnp.concatenate([my_innov, weights, jnp.pad(blocks.astype(F32), ((0, 0), (0, 128 - crossing)))], axis=1)
    own = to_all(message)

    slab_split = split_slab(cov_slab)
    send = spread(cross_cov.T)
    own, send, slab_split = lax.optimization_barrier((own, send, slab_split))
    cross = lax.all_to_all(send, "obs", 0, 0)
    other = lax.ppermute(own, "vox", SWAP)
    first_block = lax.axis_index("vox") * local_blocks
    flat = (everyone * share, -1)
    partial_own = predict(own.reshape(flat), skip, slab_split, first_block, local_blocks, crossing, block_size)
    other, partial_own = lax.optimization_barrier((other, partial_own))
    partial_other = predict(other.reshape(flat), skip, slab_split, first_block, local_blocks, crossing, block_size)

    mine = partial_own + lax.ppermute(partial_other, "vox", SWAP)
    theirs = partial_other + lax.ppermute(partial_own, "vox", SWAP)
    low = jnp.where(core == 0, mine, theirs).reshape(everyone, 1, share, columns)
    high = jnp.where(core == 0, theirs, mine).reshape(everyone, 1, share, columns)
    chip_sum = jnp.concatenate([low, high], axis=1)
    chip_sum, other = lax.optimization_barrier((chip_sum, other))
    predicted = chip_sum + lax.ppermute(chip_sum, "vox", [(0, 2), (2, 0), (1, 3), (3, 1)])
    minus = minus_inverse(core_array, own, other, skip)
    solved = solve_turned(minus, predicted)

    at_x = device % 4
    at_y = device // 8
    from_x = [lax.ppermute(solved, "obs", steps_along(2, d)) for d in (1, 3, 2)]
    from_y = [lax.ppermute(solved, "obs", steps_along(0, d)) for d in (1, 3, 2)]
    solved, from_x, from_y = lax.optimization_barrier((solved, from_x, from_y))
    parts_x = products([solved] + from_x, cross, 0)
    back_x = [lax.ppermute(part, "obs", steps_along(2, -d)) for part, d in zip(parts_x[1:], (1, 3, 2))]
    parts_y = products([solved] + from_y, cross, 1)
    back_y = [lax.ppermute(part, "obs", steps_along(0, -d)) for part, d in zip(parts_y[1:], (1, 3, 2))]
    out = downdate([at_x, 4 + at_y], [parts_x[0], parts_y[0]], cov_slab)
    out = downdate([(at_x + d) % 4 for d in (1, 3, 2)], back_x, cov_slab, out)
    return downdate([4 + (at_y + d) % 4 for d in (1, 3, 2)], back_y, cov_slab, out)


def solution(mesh):
    placed = (
        P("vox", "obs"),
        P("vox", "obs"),
        P("obs", None),
        P("obs", None),
        P("obs"),
        P("obs", None),
    )
    return jax.shard_map(
        shards, mesh=mesh, in_specs=placed, out_specs=P("vox", "obs"), check_vma=False
    )
```

```python
import functools
import math

import jax
import jax.numpy as jnp
from jax import lax
from jax.experimental import pallas as pl
from jax.experimental.pallas import tpu as pltpu
from jax.sharding import PartitionSpec as P

F32 = jnp.float32
BF16 = jnp.bfloat16
VMEM_LIMIT = 60 * 1024 * 1024


def halves(x):
    high = x.astype(BF16)
    return high, (x - high.astype(F32)).astype(BF16)


def dot(a, b):
    return jnp.dot(a, b, preferred_element_type=F32)


def dot_split(a, b):
    ah, al = halves(a)
    bh, bl = halves(b)
    return dot(ah, bh) + (dot(ah, bl) + dot(al, bh))


def split_kernel(cov_ref, out_ref):
    columns = cov_ref.shape[1]
    high, low = halves(cov_ref[...])
    out_ref[:, :columns] = high
    out_ref[:, columns:] = low


def split_slab(cov_slab):
    rows, columns = cov_slab.shape
    tile = 2048
    return pl.pallas_call(
        split_kernel,
        grid=(rows // tile,),
        in_specs=[pl.BlockSpec((tile, columns), lambda i: (i, 0))],
        out_specs=pl.BlockSpec((tile, 2 * columns), lambda i: (i, 0)),
        out_shape=jax.ShapeDtypeStruct((rows, 2 * columns), BF16),
        compiler_params=pltpu.CompilerParams(vmem_limit_bytes=VMEM_LIMIT),
        cost_estimate=pl.CostEstimate(flops=4 * rows * columns, bytes_accessed=8 * rows * columns, transcendentals=0),
        name="split",
    )(cov_slab)


def predict_kernel(place_ref, slots_ref, far_ref, out_ref, dense, split_ref, arrived, *, tile, crossing, block, skip):
    step = pl.program_id(0)
    fetch = pltpu.make_async_copy(far_ref, split_ref, arrived)
    rows, columns = split_ref.shape
    columns = columns // 2
    pairs = rows // (2 * block)
    deep = 2 * 2 * block
    quads = rows // deep
    lane = lax.broadcasted_iota(jnp.int32, (8, 2 * block), 1)
    sub = lax.broadcasted_iota(jnp.int32, (8, 2 * block), 0)
    upper = (lane >= block).astype(jnp.int32)

    @pl.when(step == 0)
    def _():
        fetch.start()

        def clear(i, c):
            dense[i] = jnp.zeros_like(dense[i])
            return c

        lax.fori_loop(0, pairs, clear, 0)

    def scatter(group, c):
        row = pl.multiple_of(group * 8, 8)
        first = (step * tile + row) * crossing
        blocks = slots_ref[pl.ds(row, 8), skip + crossing * block :].astype(jnp.int32) & 1
        for n in range(crossing):
            if n % 2 == 0:
                plain = slots_ref[pl.ds(row, 8), pl.ds(skip + n * block, 2 * block)]
                turned = pltpu.roll(plain, block, 1)
                both = jnp.where(upper == 0, plain, turned)
            else:
                both = jnp.where(upper == 0, turned, plain)
            half = blocks[:, n : n + 1] == upper
            for i in range(8):
                where = place_ref[first + i * crossing + n]
                pltpu.store(dense.at[where, pl.ds(row, 8), :], both, mask=half & (sub == i))
        return c

    lax.fori_loop(0, tile // 8, scatter, 0)
    out_ref[...] = jnp.zeros_like(out_ref)
    together = 16

    @pl.when(step == 0)
    def _():
        fetch.wait()

    def multiply(i, c):
        wide_sum = jnp.zeros((tile, 2 * columns), F32)
        small = jnp.zeros((tile, columns), F32)
        for k in range(together):
            q = i * together + k
            here = pl.ds(pl.multiple_of(q * deep, deep), deep)
            wide = jnp.concatenate([dense[2 * q], dense[2 * q + 1]], axis=1)
            high, low = halves(wide)
            wide_sum = wide_sum + dot(high, split_ref[here, :])
            small = small + dot(low, split_ref[here, :columns])
            dense[2 * q] = jnp.zeros((tile, 2 * block), F32)
            dense[2 * q + 1] = jnp.zeros((tile, 2 * block), F32)
        out_ref[...] += wide_sum[:, :columns] + (wide_sum[:, columns:] + small)
        return c

    lax.fori_loop(0, quads // together, multiply, 0)


def predict(slots, skip, slab_split, first_block, local_blocks, crossing, block):
    count, width = slots.shape
    rows, columns = slab_split.shape
    columns = columns // 2
    tile = 256
    lanes = skip + crossing * block
    blocks = slots[:, lanes : lanes + crossing].astype(jnp.int32)
    local = blocks - first_block
    inside = (local >= 0) & (local < local_blocks) & (blocks >= 0)
    place = jnp.where(inside, local // 2, local_blocks // 2).reshape(-1)
    return pl.pallas_call(
        functools.partial(predict_kernel, tile=tile, crossing=crossing, block=block, skip=skip),
        grid_spec=pltpu.PrefetchScalarGridSpec(
            num_scalar_prefetch=1,
            grid=(count // tile,),
            in_specs=[
                pl.BlockSpec((tile, width), lambda i, place: (i, 0)),
                pl.BlockSpec(memory_space=pl.ANY),
            ],
            out_specs=pl.BlockSpec((tile, columns), lambda i, place: (i, 0)),
            scratch_shapes=[
                pltpu.VMEM((rows // (2 * block) + 1, tile, 2 * block), F32),
                pltpu.VMEM((rows, 2 * columns), BF16),
                pltpu.SemaphoreType.DMA,
            ],
        ),
        out_shape=jax.ShapeDtypeStruct((count, columns), F32),
        compiler_params=pltpu.CompilerParams(vmem_limit_bytes=VMEM_LIMIT),
        cost_estimate=pl.CostEstimate(
            flops=12 * count * rows * columns, bytes_accessed=rows * columns * 4, transcendentals=0
        ),
        name="predict",
    )(place, slots, slab_split)


def spread_lane(rows, lane):
    return jnp.take_along_axis(rows, jnp.full(rows.shape, lane, jnp.int32), axis=1)


def sweep_rows(rows, first):
    sub = lax.broadcasted_iota(jnp.int32, rows.shape, 0)
    lane = lax.broadcasted_iota(jnp.int32, rows.shape, 1) - first
    cols = [spread_lane(rows, first + j) for j in range(8)]

    def row(v, p):
        return jnp.broadcast_to(v[p : p + 1, :], rows.shape)

    out = rows
    for p in range(0, 8, 2):
        q = p + 1
        a, b, d = row(cols[p], p), row(cols[q], p), row(cols[q], q)
        inv = 1.0 / (a * d - b * b)
        a, b, d = a * inv, b * inv, d * inv
        out = jnp.where((lane == p) | (lane == q), jnp.where(sub == lane, 1.0, 0.0), out)

        def eliminate(v):
            at_p, at_q = row(v, p), row(v, q)
            new_p = d * at_p - b * at_q
            new_q = a * at_q - b * at_p
            rest = v - cols[p] * new_p - cols[q] * new_q
            return jnp.where(sub == p, new_p, jnp.where(sub == q, new_q, rest))

        out = eliminate(out)
        cols = [eliminate(col) if j > q else col for j, col in enumerate(cols)]
    return jnp.where((lane >= 0) & (lane < 8), -out, out)


def take_away(rows, swept, first):
    lanes = lax.broadcasted_iota(jnp.int32, rows.shape, 1)
    count = swept.shape[0]
    even = jnp.where((lanes >= first) & (lanes < first + count), 0.0, rows)
    odd = jnp.zeros_like(rows)
    for j in range(0, count, 2):
        even = even - spread_lane(rows, first + j) * swept[j : j + 1, :]
        odd = odd + spread_lane(rows, first + j + 1) * swept[j + 1 : j + 2, :]
    return even - odd


def small_sweep(block):
    size = block.shape[0]
    strip = 16
    all_lanes = lax.broadcasted_iota(jnp.int32, (size, size), 1)
    rows = [block[at : at + 8, :] for at in range(0, strip, 8)]
    for base in range(0, size, strip):
        for g in range(strip // 8):
            top = sweep_rows(rows[g], base + 8 * g)
            rows = [top if e == g else take_away(rows[e], top, base + 8 * g) for e in range(strip // 8)]
        middle = jnp.concatenate(rows, axis=0)
        after = base + strip
        ahead = [take_away(block[at : at + 8, :], middle, base) for at in range(after, min(after + strip, size), 8)]
        above = [jnp.zeros((base, size), F32)] if base else []
        below = [jnp.zeros((size - after, size), F32)] if after < size else []
        high, low = halves(jnp.concatenate(above + [middle] + below, axis=0))
        block_high, block_low = halves(block)
        keep = jnp.where((all_lanes >= base) & (all_lanes < after), 0.0, block)
        new = keep - (
            dot(jnp.concatenate([block_high, block_low], axis=1), jnp.concatenate([high, high], axis=0))
            + dot(block_high, low)
        )
        above = [new[:base]] if base else []
        below = [new[after + strip :]] if after + strip < size else []
        block = jnp.concatenate(above + [middle] + ahead + below, axis=0)
        rows = ahead
    return block


def inverse_kernel(core_ref, own_ref, other_ref, m_ref, left, right, pivot, *, size):
    n = m_ref.shape[0]
    regions, share, lanes = own_ref.shape
    core = core_ref[0]
    blocks = n // size
    per_block = regions // blocks

    def place(i, c):
        mine = pl.multiple_of((2 * i + core) * share, share)
        theirs = pl.multiple_of((2 * i + 1 - core) * share, share)
        for j in range(lanes // size):
            at = pl.ds(pl.multiple_of(lax.rem(lax.div(i, per_block) + j, blocks) * size, size), size)
            m_ref[pl.ds(mine, share), at] = own_ref[i, :, j * size : (j + 1) * size]
            m_ref[pl.ds(theirs, share), at] = other_ref[i, :, j * size : (j + 1) * size]
        return c

    lax.fori_loop(0, regions, place, 0)

    def mirror(i, c):
        at = pl.ds(pl.multiple_of(i * size, size), size)
        for j in range(1, blocks - lanes // size + 1):
            to = pl.ds(pl.multiple_of(lax.rem(i + j, blocks) * size, size), size)
            m_ref[to, at] = m_ref[at, to].T
        return c

    lax.fori_loop(0, blocks, mirror, 0)

    def sweep(k, c):
        at = pl.ds(pl.multiple_of(k * size, size), size)
        minus = small_sweep(m_ref[at, at])
        pivot[...] = dot_split(minus, m_ref[at, :]) * -1.0
        pivot[:, at] = minus
        high, low = halves(m_ref[:, at])
        left[:, :size] = high
        left[:, size:] = low
        m_ref[:, at] = jnp.zeros((n, size), F32)
        high, low = halves(pivot[...])
        right[:size, :] = high
        right[size : 2 * size, :] = high
        right[2 * size :, :] = low
        product = dot(left[...], right[: 2 * size, :]) + dot(left[:, :size], right[2 * size :, :])
        m_ref[...] = m_ref[...] - product
        m_ref[at, :] = pivot[...]
        return c

    lax.fori_loop(0, n // size, sweep, 0)


def minus_inverse(core, own, other, lanes):
    regions, share, _ = own.shape
    n = 2 * regions * share
    size = 128
    return pl.pallas_call(
        functools.partial(inverse_kernel, size=size),
        grid=(1,),
        in_specs=[pl.BlockSpec(memory_space=pltpu.SMEM)]
        + [pl.BlockSpec((regions, share, lanes), lambda i: (0, 0, 0))] * 2,
        out_specs=pl.BlockSpec(memory_space=pltpu.VMEM),
        out_shape=jax.ShapeDtypeStruct((n, n), F32),
        scratch_shapes=[
            pltpu.VMEM((n, 2 * size), BF16),
            pltpu.VMEM((3 * size, n), BF16),
            pltpu.VMEM((size, n), F32),
        ],
        compiler_params=pltpu.CompilerParams(vmem_limit_bytes=VMEM_LIMIT),
        cost_estimate=pl.CostEstimate(flops=60 * n * n * n, bytes_accessed=8 * n * n, transcendentals=0),
        name="minus_inverse",
    )(core, own, other)


def solve_kernel(minus_ref, here_ref, there_ref, out_ref):
    predicted = (here_ref[...] + there_ref[...]).reshape(minus_ref.shape[0], -1)
    out_ref[...] = (-dot_split(predicted.T, minus_ref[...])).astype(BF16)


def solve_turned(minus, here, there):
    n, columns = minus.shape[0], here.shape[-1]
    return pl.pallas_call(
        solve_kernel,
        in_specs=[pl.BlockSpec(memory_space=pltpu.VMEM)] * 3,
        out_specs=pl.BlockSpec(memory_space=pltpu.VMEM),
        out_shape=jax.ShapeDtypeStruct((columns, n), BF16),
        compiler_params=pltpu.CompilerParams(vmem_limit_bytes=VMEM_LIMIT),
        cost_estimate=pl.CostEstimate(flops=6 * n * n * columns, bytes_accessed=4 * n * n, transcendentals=0),
        name="solve",
    )(minus, here, there)


def spread_kernel(by_x_ref, by_y_ref, out_ref):
    out_ref[0, 0] = by_x_ref[...]
    out_ref[0, 1] = by_y_ref[...]


def spread(turned):
    slots, rows = turned.shape
    width = rows // 8
    everyone = math.prod(SIZES)
    return pl.pallas_call(
        spread_kernel,
        grid=(everyone,),
        in_specs=[
            pl.BlockSpec((slots, width), lambda i: (0, i % 4)),
            pl.BlockSpec((slots, width), lambda i: (0, 4 + i // 8)),
        ],
        out_specs=pl.BlockSpec((1, 2, slots, width), lambda i: (i, 0, 0, 0)),
        out_shape=jax.ShapeDtypeStruct((everyone, 2, slots, width), turned.dtype),
        compiler_params=pltpu.CompilerParams(vmem_limit_bytes=VMEM_LIMIT),
        cost_estimate=pl.CostEstimate(flops=0, bytes_accessed=16 * slots * rows, transcendentals=0),
        name="spread",
    )(turned, turned)


def product_kernel(*refs, members):
    solved_refs, cross_ref, out_refs, stack = refs[:members], refs[members], refs[members + 1 : -1], refs[-1]
    columns = solved_refs[0].shape[0]

    @pl.when(pl.program_id(0) == 0)
    def _():
        for i, ref in enumerate(solved_refs):
            stack[i * columns : (i + 1) * columns, :] = ref[...]

    everyone, _, slots, tile = cross_ref.shape
    product = dot(stack[...], cross_ref[...].reshape(everyone * slots, tile))
    for i, ref in enumerate(out_refs):
        ref[...] = product[i * columns : (i + 1) * columns, :].astype(ref.dtype)


def products(solved, cross, half):
    members = len(solved)
    columns, n = solved[0].shape
    everyone, _, slots, width = cross.shape
    tile = 1024
    return pl.pallas_call(
        functools.partial(product_kernel, members=members),
        grid=(width // tile,),
        in_specs=[pl.BlockSpec(memory_space=pltpu.VMEM)] * members
        + [pl.BlockSpec((everyone, 1, slots, tile), lambda i: (0, half, 0, i))],
        out_specs=[pl.BlockSpec((columns, tile), lambda i: (0, i))] * members,
        out_shape=[jax.ShapeDtypeStruct((columns, width), BF16 if i else F32) for i in range(members)],
        scratch_shapes=[pltpu.VMEM((members * columns, n), BF16)],
        compiler_params=pltpu.CompilerParams(vmem_limit_bytes=VMEM_LIMIT),
        cost_estimate=pl.CostEstimate(
            flops=2 * members * columns * n * width, bytes_accessed=2 * n * width, transcendentals=0
        ),
        name="products",
    )(*solved, cross)


def downdate_kernel(chunk_ref, *refs, count):
    product_refs, cov_ref, out_ref = refs[:count], refs[count], refs[-1]
    for i, ref in enumerate(product_refs):

        @pl.when(pl.program_id(0) == i)
        def _():
            out_ref[...] = cov_ref[...] - ref[...].T.astype(F32)


def downdate(chunks, parts, cov_slab, so_far=None):
    rows, columns = cov_slab.shape
    count = len(parts)
    tile = parts[0].shape[1]
    spec = pl.BlockSpec((tile, columns), lambda i, chunk: (chunk[i], 0))
    more = [] if so_far is None else [so_far]
    return pl.pallas_call(
        functools.partial(downdate_kernel, count=count),
        grid_spec=pltpu.PrefetchScalarGridSpec(
            num_scalar_prefetch=1,
            grid=(count,),
            in_specs=[pl.BlockSpec(memory_space=pltpu.VMEM)] * count
            + [spec]
            + [pl.BlockSpec(memory_space=pl.ANY)] * len(more),
            out_specs=spec,
        ),
        out_shape=jax.ShapeDtypeStruct((rows, columns), F32),
        input_output_aliases={count + 2: 0} if more else {},
        compiler_params=pltpu.CompilerParams(vmem_limit_bytes=VMEM_LIMIT),
        cost_estimate=pl.CostEstimate(
            flops=count * tile * columns, bytes_accessed=10 * count * tile * columns, transcendentals=0
        ),
        name="downdate",
    )(jnp.stack(chunks).astype(jnp.int32), *parts, cov_slab, *more)


def merged(ray_blocks, weights):
    slots, crossing = ray_blocks.shape
    same = ray_blocks[:, :, None] == ray_blocks[:, None, :]
    order = jnp.arange(crossing, dtype=jnp.int32)
    first = ~jnp.any(same & (order[None, None, :] < order[None, :, None]), axis=2)
    parts = weights.reshape(slots, crossing, -1)
    total = jnp.sum(jnp.where(same[:, :, :, None], parts[:, None, :, :], 0.0), axis=2)
    return jnp.where(first, ray_blocks, -1), total.reshape(weights.shape)


SIZES = (4, 2, 4)
SWAP = [(0, 1), (1, 0), (2, 3), (3, 2)]


def steps_along(axis, distance):
    pairs = []
    for y in range(SIZES[0]):
        for z in range(SIZES[1]):
            for x in range(SIZES[2]):
                to = [y, z, x]
                to[axis] = (to[axis] + distance) % SIZES[axis]
                pairs.append(((y * SIZES[1] + z) * SIZES[2] + x, (to[0] * SIZES[1] + to[1]) * SIZES[2] + to[2]))
    return pairs


def to_all(piece):
    everyone = math.prod(SIZES)
    return lax.all_to_all(jnp.broadcast_to(piece[None], (everyone,) + piece.shape), "obs", 0, 0)


def shards(cov_slab, cross_cov, ray_blocks, ray_coeff, region_rows, innov_cov):
    local_rows, columns = cov_slab.shape
    slot_count, crossing = ray_blocks.shape
    block_size = ray_coeff.shape[1] // crossing
    local_blocks = local_rows // block_size
    everyone = math.prod(SIZES)
    device = lax.axis_index("obs")
    core = lax.axis_index("vox") % 2
    core_array = core.astype(jnp.int32).reshape(1)
    share = slot_count // 2
    start = core * share

    my_blocks = lax.dynamic_slice_in_dim(ray_blocks, start, share, 0)
    my_coeff = lax.dynamic_slice_in_dim(ray_coeff, start, share, 0)
    live = start + jnp.arange(share, dtype=jnp.int32) < region_rows[0]
    weights = jnp.where(live[:, None], my_coeff, 0.0)
    blocks, weights = merged(my_blocks, weights)
    my_innov = lax.dynamic_slice_in_dim(innov_cov, start, share, 0)
    skip = 640
    my_innov = lax.dynamic_slice_in_dim(jnp.concatenate([my_innov, my_innov], axis=1), device // 4 * 128, skip, 1)
    message = jnp.concatenate([my_innov, weights, jnp.pad(blocks.astype(F32), ((0, 0), (0, 128 - crossing)))], axis=1)
    own = to_all(message)

    slab_split = split_slab(cov_slab)
    send = spread(cross_cov.T)
    own, send, slab_split = lax.optimization_barrier((own, send, slab_split))
    cross = lax.all_to_all(send, "obs", 0, 0)
    other = lax.ppermute(own, "vox", SWAP)
    first_block = lax.axis_index("vox") * local_blocks
    flat = (everyone * share, -1)
    partial_own = predict(own.reshape(flat), skip, slab_split, first_block, local_blocks, crossing, block_size)
    other, partial_own = lax.optimization_barrier((other, partial_own))
    partial_other = predict(other.reshape(flat), skip, slab_split, first_block, local_blocks, crossing, block_size)

    mine = partial_own + lax.ppermute(partial_other, "vox", SWAP)
    theirs = partial_other + lax.ppermute(partial_own, "vox", SWAP)
    low = jnp.where(core == 0, mine, theirs).reshape(everyone, 1, share, columns)
    high = jnp.where(core == 0, theirs, mine).reshape(everyone, 1, share, columns)
    chip_sum = jnp.concatenate([low, high], axis=1)
    chip_sum, other = lax.optimization_barrier((chip_sum, other))
    there = lax.ppermute(chip_sum, "vox", [(0, 2), (2, 0), (1, 3), (3, 1)])
    minus = minus_inverse(core_array, own, other, skip)
    solved = solve_turned(minus, chip_sum, there)

    at_x = device % 4
    at_y = device // 8
    from_x = [lax.ppermute(solved, "obs", steps_along(2, d)) for d in (2, 1, 3)]
    from_y = [lax.ppermute(solved, "obs", steps_along(0, d)) for d in (2, 1, 3)]
    solved, from_x, from_y = lax.optimization_barrier((solved, from_x, from_y))
    parts_x = products([solved] + from_x, cross, 0)
    back_x = [lax.ppermute(part, "obs", steps_along(2, -d)) for part, d in zip(parts_x[1:], (2, 1, 3))]
    parts_y = products([solved] + from_y, cross, 1)
    back_y = [lax.ppermute(part, "obs", steps_along(0, -d)) for part, d in zip(parts_y[1:], (2, 1, 3))]
    out = downdate([at_x, 4 + at_y], [parts_x[0], parts_y[0]], cov_slab)
    out = downdate([(at_x + d) % 4 for d in (2, 1, 3)], back_x, cov_slab, out)
    return downdate([4 + (at_y + d) % 4 for d in (2, 1, 3)], back_y, cov_slab, out)


def solution(mesh):
    placed = (
        P("vox", "obs"),
        P("vox", "obs"),
        P("obs", None),
        P("obs", None),
        P("obs"),
        P("obs", None),
    )
    return jax.shard_map(
        shards, mesh=mesh, in_specs=placed, out_specs=P("vox", "obs"), check_vma=False
    )
```

```python
import functools
import math

import jax
import jax.numpy as jnp
from jax import lax
from jax.experimental import pallas as pl
from jax.experimental.pallas import tpu as pltpu
from jax.sharding import PartitionSpec as P

F32 = jnp.float32
BF16 = jnp.bfloat16
VMEM_LIMIT = 60 * 1024 * 1024


def halves(x):
    high = x.astype(BF16)
    return high, (x - high.astype(F32)).astype(BF16)


def dot(a, b):
    return jnp.dot(a, b, preferred_element_type=F32)


def dot_split(a, b):
    ah, al = halves(a)
    bh, bl = halves(b)
    return dot(ah, bh) + (dot(ah, bl) + dot(al, bh))


def split_kernel(cov_ref, out_ref):
    columns = cov_ref.shape[1]
    high, low = halves(cov_ref[...])
    out_ref[:, :columns] = high
    out_ref[:, columns:] = low


def split_slab(cov_slab):
    rows, columns = cov_slab.shape
    tile = 2048
    return pl.pallas_call(
        split_kernel,
        grid=(rows // tile,),
        in_specs=[pl.BlockSpec((tile, columns), lambda i: (i, 0))],
        out_specs=pl.BlockSpec((tile, 2 * columns), lambda i: (i, 0)),
        out_shape=jax.ShapeDtypeStruct((rows, 2 * columns), BF16),
        compiler_params=pltpu.CompilerParams(vmem_limit_bytes=VMEM_LIMIT),
        cost_estimate=pl.CostEstimate(flops=4 * rows * columns, bytes_accessed=8 * rows * columns, transcendentals=0),
        name="split",
    )(cov_slab)


def predict_kernel(place_ref, slots_ref, far_ref, out_ref, dense, split_ref, arrived, *, tile, crossing, block, skip):
    step = pl.program_id(0)
    fetch = pltpu.make_async_copy(far_ref, split_ref, arrived)
    rows, columns = split_ref.shape
    columns = columns // 2
    pairs = rows // (2 * block)
    deep = 2 * 2 * block
    quads = rows // deep
    lane = lax.broadcasted_iota(jnp.int32, (8, 2 * block), 1)
    sub = lax.broadcasted_iota(jnp.int32, (8, 2 * block), 0)
    upper = (lane >= block).astype(jnp.int32)

    @pl.when(step == 0)
    def _():
        fetch.start()

        def clear(i, c):
            dense[i] = jnp.zeros_like(dense[i])
            return c

        lax.fori_loop(0, pairs, clear, 0)

    def scatter(group, c):
        row = pl.multiple_of(group * 8, 8)
        first = (step * tile + row) * crossing
        blocks = slots_ref[pl.ds(row, 8), skip + crossing * block :].astype(jnp.int32) & 1
        for n in range(crossing):
            if n % 2 == 0:
                plain = slots_ref[pl.ds(row, 8), pl.ds(skip + n * block, 2 * block)]
                turned = pltpu.roll(plain, block, 1)
                both = jnp.where(upper == 0, plain, turned)
            else:
                both = jnp.where(upper == 0, turned, plain)
            half = blocks[:, n : n + 1] == upper
            for i in range(8):
                where = place_ref[first + i * crossing + n]
                pltpu.store(dense.at[where, pl.ds(row, 8), :], both, mask=half & (sub == i))
        return c

    lax.fori_loop(0, tile // 8, scatter, 0)
    out_ref[...] = jnp.zeros_like(out_ref)
    together = 32

    @pl.when(step == 0)
    def _():
        fetch.wait()

    def multiply(i, c):
        wide_sum = jnp.zeros((tile, 2 * columns), F32)
        small = jnp.zeros((tile, columns), F32)
        for k in range(together):
            q = i * together + k
            here = pl.ds(pl.multiple_of(q * deep, deep), deep)
            wide = jnp.concatenate([dense[2 * q], dense[2 * q + 1]], axis=1)
            high, low = halves(wide)
            wide_sum = wide_sum + dot(high, split_ref[here, :])
            small = small + dot(low, split_ref[here, :columns])
            dense[2 * q] = jnp.zeros((tile, 2 * block), F32)
            dense[2 * q + 1] = jnp.zeros((tile, 2 * block), F32)
        out_ref[...] += wide_sum[:, :columns] + (wide_sum[:, columns:] + small)
        return c

    lax.fori_loop(0, quads // together, multiply, 0)


def predict(slots, skip, slab_split, first_block, local_blocks, crossing, block):
    count, width = slots.shape
    rows, columns = slab_split.shape
    columns = columns // 2
    tile = 256
    lanes = skip + crossing * block
    blocks = slots[:, lanes : lanes + crossing].astype(jnp.int32)
    local = blocks - first_block
    inside = (local >= 0) & (local < local_blocks) & (blocks >= 0)
    place = jnp.where(inside, local // 2, local_blocks // 2).reshape(-1)
    return pl.pallas_call(
        functools.partial(predict_kernel, tile=tile, crossing=crossing, block=block, skip=skip),
        grid_spec=pltpu.PrefetchScalarGridSpec(
            num_scalar_prefetch=1,
            grid=(count // tile,),
            in_specs=[
                pl.BlockSpec((tile, width), lambda i, place: (i, 0)),
                pl.BlockSpec(memory_space=pl.ANY),
            ],
            out_specs=pl.BlockSpec((tile, columns), lambda i, place: (i, 0)),
            scratch_shapes=[
                pltpu.VMEM((rows // (2 * block) + 1, tile, 2 * block), F32),
                pltpu.VMEM((rows, 2 * columns), BF16),
                pltpu.SemaphoreType.DMA,
            ],
        ),
        out_shape=jax.ShapeDtypeStruct((count, columns), F32),
        compiler_params=pltpu.CompilerParams(vmem_limit_bytes=VMEM_LIMIT),
        cost_estimate=pl.CostEstimate(
            flops=12 * count * rows * columns, bytes_accessed=rows * columns * 4, transcendentals=0
        ),
        name="predict",
    )(place, slots, slab_split)


def spread_lane(rows, lane):
    return jnp.take_along_axis(rows, jnp.full(rows.shape, lane, jnp.int32), axis=1)


def sweep_rows(rows, first):
    sub = lax.broadcasted_iota(jnp.int32, rows.shape, 0)
    lane = lax.broadcasted_iota(jnp.int32, rows.shape, 1) - first
    cols = [spread_lane(rows, first + j) for j in range(8)]

    def row(v, p):
        return jnp.broadcast_to(v[p : p + 1, :], rows.shape)

    out = rows
    for p in range(0, 8, 2):
        q = p + 1
        a, b, d = row(cols[p], p), row(cols[q], p), row(cols[q], q)
        inv = 1.0 / (a * d - b * b)
        a, b, d = a * inv, b * inv, d * inv
        out = jnp.where((lane == p) | (lane == q), jnp.where(sub == lane, 1.0, 0.0), out)

        def eliminate(v):
            at_p, at_q = row(v, p), row(v, q)
            new_p = d * at_p - b * at_q
            new_q = a * at_q - b * at_p
            rest = v - cols[p] * new_p - cols[q] * new_q
            return jnp.where(sub == p, new_p, jnp.where(sub == q, new_q, rest))

        out = eliminate(out)
        cols = [eliminate(col) if j > q else col for j, col in enumerate(cols)]
    return jnp.where((lane >= 0) & (lane < 8), -out, out)


def take_away(rows, swept, first):
    lanes = lax.broadcasted_iota(jnp.int32, rows.shape, 1)
    count = swept.shape[0]
    even = jnp.where((lanes >= first) & (lanes < first + count), 0.0, rows)
    odd = jnp.zeros_like(rows)
    for j in range(0, count, 2):
        even = even - spread_lane(rows, first + j) * swept[j : j + 1, :]
        odd = odd + spread_lane(rows, first + j + 1) * swept[j + 1 : j + 2, :]
    return even - odd


def small_sweep(block):
    size = block.shape[0]
    strip = 16
    all_lanes = lax.broadcasted_iota(jnp.int32, (size, size), 1)
    rows = [block[at : at + 8, :] for at in range(0, strip, 8)]
    for base in range(0, size, strip):
        for g in range(strip // 8):
            top = sweep_rows(rows[g], base + 8 * g)
            rows = [top if e == g else take_away(rows[e], top, base + 8 * g) for e in range(strip // 8)]
        middle = jnp.concatenate(rows, axis=0)
        after = base + strip
        ahead = [take_away(block[at : at + 8, :], middle, base) for at in range(after, min(after + strip, size), 8)]
        above = [jnp.zeros((base, size), F32)] if base else []
        below = [jnp.zeros((size - after, size), F32)] if after < size else []
        high, low = halves(jnp.concatenate(above + [middle] + below, axis=0))
        block_high, block_low = halves(block)
        keep = jnp.where((all_lanes >= base) & (all_lanes < after), 0.0, block)
        new = keep - (
            dot(jnp.concatenate([block_high, block_low], axis=1), jnp.concatenate([high, high], axis=0))
            + dot(block_high, low)
        )
        above = [new[:base]] if base else []
        below = [new[after + strip :]] if after + strip < size else []
        block = jnp.concatenate(above + [middle] + ahead + below, axis=0)
        rows = ahead
    return block


def inverse_kernel(core_ref, own_ref, other_ref, m_ref, left, right, pivot, *, size):
    n = m_ref.shape[0]
    regions, share, lanes = own_ref.shape
    core = core_ref[0]
    blocks = n // size
    per_block = regions // blocks

    def place(i, c):
        mine = pl.multiple_of((2 * i + core) * share, share)
        theirs = pl.multiple_of((2 * i + 1 - core) * share, share)
        for j in range(lanes // size):
            at = pl.ds(pl.multiple_of(lax.rem(lax.div(i, per_block) + j, blocks) * size, size), size)
            m_ref[pl.ds(mine, share), at] = own_ref[i, :, j * size : (j + 1) * size]
            m_ref[pl.ds(theirs, share), at] = other_ref[i, :, j * size : (j + 1) * size]
        return c

    lax.fori_loop(0, regions, place, 0)

    def mirror(i, c):
        at = pl.ds(pl.multiple_of(i * size, size), size)
        for j in range(1, blocks - lanes // size + 1):
            to = pl.ds(pl.multiple_of(lax.rem(i + j, blocks) * size, size), size)
            m_ref[to, at] = m_ref[at, to].T
        return c

    lax.fori_loop(0, blocks, mirror, 0)

    def sweep(k, c):
        at = pl.ds(pl.multiple_of(k * size, size), size)
        minus = small_sweep(m_ref[at, at])
        pivot[...] = dot_split(minus, m_ref[at, :]) * -1.0
        pivot[:, at] = minus
        high, low = halves(m_ref[:, at])
        left[:, :size] = high
        left[:, size:] = low
        m_ref[:, at] = jnp.zeros((n, size), F32)
        high, low = halves(pivot[...])
        right[:size, :] = high
        right[size : 2 * size, :] = high
        right[2 * size :, :] = low
        product = dot(left[...], right[: 2 * size, :]) + dot(left[:, :size], right[2 * size :, :])
        m_ref[...] = m_ref[...] - product
        m_ref[at, :] = pivot[...]
        return c

    lax.fori_loop(0, n // size, sweep, 0)


def minus_inverse(core, own, other, lanes):
    regions, share, _ = own.shape
    n = 2 * regions * share
    size = 128
    return pl.pallas_call(
        functools.partial(inverse_kernel, size=size),
        grid=(1,),
        in_specs=[pl.BlockSpec(memory_space=pltpu.SMEM)]
        + [pl.BlockSpec((regions, share, lanes), lambda i: (0, 0, 0))] * 2,
        out_specs=pl.BlockSpec(memory_space=pltpu.VMEM),
        out_shape=jax.ShapeDtypeStruct((n, n), F32),
        scratch_shapes=[
            pltpu.VMEM((n, 2 * size), BF16),
            pltpu.VMEM((3 * size, n), BF16),
            pltpu.VMEM((size, n), F32),
        ],
        compiler_params=pltpu.CompilerParams(vmem_limit_bytes=VMEM_LIMIT),
        cost_estimate=pl.CostEstimate(flops=60 * n * n * n, bytes_accessed=8 * n * n, transcendentals=0),
        name="minus_inverse",
    )(core, own, other)


def solve_kernel(minus_ref, here_ref, there_ref, out_ref):
    predicted = (here_ref[...] + there_ref[...]).reshape(minus_ref.shape[0], -1)
    out_ref[...] = (-dot_split(predicted.T, minus_ref[...])).astype(BF16)


def solve_turned(minus, here, there):
    n, columns = minus.shape[0], here.shape[-1]
    return pl.pallas_call(
        solve_kernel,
        in_specs=[pl.BlockSpec(memory_space=pltpu.VMEM)] * 3,
        out_specs=pl.BlockSpec(memory_space=pltpu.VMEM),
        out_shape=jax.ShapeDtypeStruct((columns, n), BF16),
        compiler_params=pltpu.CompilerParams(vmem_limit_bytes=VMEM_LIMIT),
        cost_estimate=pl.CostEstimate(flops=6 * n * n * columns, bytes_accessed=4 * n * n, transcendentals=0),
        name="solve",
    )(minus, here, there)


def spread_kernel(by_x_ref, by_y_ref, out_ref):
    out_ref[0, 0] = by_x_ref[...]
    out_ref[0, 1] = by_y_ref[...]


def spread(turned):
    slots, rows = turned.shape
    width = rows // 8
    everyone = math.prod(SIZES)
    return pl.pallas_call(
        spread_kernel,
        grid=(everyone,),
        in_specs=[
            pl.BlockSpec((slots, width), lambda i: (0, i % 4)),
            pl.BlockSpec((slots, width), lambda i: (0, 4 + i // 8)),
        ],
        out_specs=pl.BlockSpec((1, 2, slots, width), lambda i: (i, 0, 0, 0)),
        out_shape=jax.ShapeDtypeStruct((everyone, 2, slots, width), turned.dtype),
        compiler_params=pltpu.CompilerParams(vmem_limit_bytes=VMEM_LIMIT),
        cost_estimate=pl.CostEstimate(flops=0, bytes_accessed=16 * slots * rows, transcendentals=0),
        name="spread",
    )(turned, turned)


def product_kernel(*refs, members):
    solved_refs, cross_ref, out_refs, stack = refs[:members], refs[members], refs[members + 1 : -1], refs[-1]
    columns = solved_refs[0].shape[0]

    @pl.when(pl.program_id(0) == 0)
    def _():
        for i, ref in enumerate(solved_refs):
            stack[i * columns : (i + 1) * columns, :] = ref[...]

    everyone, _, slots, tile = cross_ref.shape
    product = dot(stack[...], cross_ref[...].reshape(everyone * slots, tile))
    for i, ref in enumerate(out_refs):
        ref[...] = product[i * columns : (i + 1) * columns, :].astype(ref.dtype)


def products(solved, cross, half):
    members = len(solved)
    columns, n = solved[0].shape
    everyone, _, slots, width = cross.shape
    tile = 1024
    return pl.pallas_call(
        functools.partial(product_kernel, members=members),
        grid=(width // tile,),
        in_specs=[pl.BlockSpec(memory_space=pltpu.VMEM)] * members
        + [pl.BlockSpec((everyone, 1, slots, tile), lambda i: (0, half, 0, i))],
        out_specs=[pl.BlockSpec((columns, tile), lambda i: (0, i))] * members,
        out_shape=[jax.ShapeDtypeStruct((columns, width), BF16 if i else F32) for i in range(members)],
        scratch_shapes=[pltpu.VMEM((members * columns, n), BF16)],
        compiler_params=pltpu.CompilerParams(vmem_limit_bytes=VMEM_LIMIT),
        cost_estimate=pl.CostEstimate(
            flops=2 * members * columns * n * width, bytes_accessed=2 * n * width, transcendentals=0
        ),
        name="products",
    )(*solved, cross)


def downdate_kernel(chunk_ref, *refs, count):
    product_refs, cov_ref, out_ref = refs[:count], refs[count], refs[-1]
    for i, ref in enumerate(product_refs):

        @pl.when(pl.program_id(0) == i)
        def _():
            out_ref[...] = cov_ref[...] - ref[...].T.astype(F32)


def downdate(chunks, parts, cov_slab, so_far=None):
    rows, columns = cov_slab.shape
    count = len(parts)
    tile = parts[0].shape[1]
    spec = pl.BlockSpec((tile, columns), lambda i, chunk: (chunk[i], 0))
    more = [] if so_far is None else [so_far]
    return pl.pallas_call(
        functools.partial(downdate_kernel, count=count),
        grid_spec=pltpu.PrefetchScalarGridSpec(
            num_scalar_prefetch=1,
            grid=(count,),
            in_specs=[pl.BlockSpec(memory_space=pltpu.VMEM)] * count
            + [spec]
            + [pl.BlockSpec(memory_space=pl.ANY)] * len(more),
            out_specs=spec,
        ),
        out_shape=jax.ShapeDtypeStruct((rows, columns), F32),
        input_output_aliases={count + 2: 0} if more else {},
        compiler_params=pltpu.CompilerParams(vmem_limit_bytes=VMEM_LIMIT),
        cost_estimate=pl.CostEstimate(
            flops=count * tile * columns, bytes_accessed=10 * count * tile * columns, transcendentals=0
        ),
        name="downdate",
    )(jnp.stack(chunks).astype(jnp.int32), *parts, cov_slab, *more)


def merged(ray_blocks, weights):
    slots, crossing = ray_blocks.shape
    same = ray_blocks[:, :, None] == ray_blocks[:, None, :]
    order = jnp.arange(crossing, dtype=jnp.int32)
    first = ~jnp.any(same & (order[None, None, :] < order[None, :, None]), axis=2)
    parts = weights.reshape(slots, crossing, -1)
    total = jnp.sum(jnp.where(same[:, :, :, None], parts[:, None, :, :], 0.0), axis=2)
    return jnp.where(first, ray_blocks, -1), total.reshape(weights.shape)


SIZES = (4, 2, 4)
SWAP = [(0, 1), (1, 0), (2, 3), (3, 2)]


def steps_along(axis, distance):
    pairs = []
    for y in range(SIZES[0]):
        for z in range(SIZES[1]):
            for x in range(SIZES[2]):
                to = [y, z, x]
                to[axis] = (to[axis] + distance) % SIZES[axis]
                pairs.append(((y * SIZES[1] + z) * SIZES[2] + x, (to[0] * SIZES[1] + to[1]) * SIZES[2] + to[2]))
    return pairs


def to_all(piece):
    everyone = math.prod(SIZES)
    return lax.all_to_all(jnp.broadcast_to(piece[None], (everyone,) + piece.shape), "obs", 0, 0)


def shards(cov_slab, cross_cov, ray_blocks, ray_coeff, region_rows, innov_cov):
    local_rows, columns = cov_slab.shape
    slot_count, crossing = ray_blocks.shape
    block_size = ray_coeff.shape[1] // crossing
    local_blocks = local_rows // block_size
    everyone = math.prod(SIZES)
    device = lax.axis_index("obs")
    core = lax.axis_index("vox") % 2
    core_array = core.astype(jnp.int32).reshape(1)
    share = slot_count // 2
    start = core * share

    my_blocks = lax.dynamic_slice_in_dim(ray_blocks, start, share, 0)
    my_coeff = lax.dynamic_slice_in_dim(ray_coeff, start, share, 0)
    live = start + jnp.arange(share, dtype=jnp.int32) < region_rows[0]
    weights = jnp.where(live[:, None], my_coeff, 0.0)
    blocks, weights = merged(my_blocks, weights)
    my_innov = lax.dynamic_slice_in_dim(innov_cov, start, share, 0)
    skip = 640
    my_innov = lax.dynamic_slice_in_dim(jnp.concatenate([my_innov, my_innov], axis=1), device // 4 * 128, skip, 1)
    message = jnp.concatenate([my_innov, weights, jnp.pad(blocks.astype(F32), ((0, 0), (0, 128 - crossing)))], axis=1)
    own = to_all(message)

    slab_split = split_slab(cov_slab)
    send = spread(cross_cov.T)
    own, send, slab_split = lax.optimization_barrier((own, send, slab_split))
    cross = lax.all_to_all(send, "obs", 0, 0)
    other = lax.ppermute(own, "vox", SWAP)
    first_block = lax.axis_index("vox") * local_blocks
    flat = (everyone * share, -1)
    partial_own = predict(own.reshape(flat), skip, slab_split, first_block, local_blocks, crossing, block_size)
    other, partial_own = lax.optimization_barrier((other, partial_own))
    partial_other = predict(other.reshape(flat), skip, slab_split, first_block, local_blocks, crossing, block_size)

    mine = partial_own + lax.ppermute(partial_other, "vox", SWAP)
    theirs = partial_other + lax.ppermute(partial_own, "vox", SWAP)
    low = jnp.where(core == 0, mine, theirs).reshape(everyone, 1, share, columns)
    high = jnp.where(core == 0, theirs, mine).reshape(everyone, 1, share, columns)
    chip_sum = jnp.concatenate([low, high], axis=1)
    chip_sum, other = lax.optimization_barrier((chip_sum, other))
    there = lax.ppermute(chip_sum, "vox", [(0, 2), (2, 0), (1, 3), (3, 1)])
    minus = minus_inverse(core_array, own, other, skip)
    solved = solve_turned(minus, chip_sum, there)

    at_x = device % 4
    at_y = device // 8
    from_x = [lax.ppermute(solved, "obs", steps_along(2, d)) for d in (2, 1, 3)]
    from_y = [lax.ppermute(solved, "obs", steps_along(0, d)) for d in (2, 1, 3)]
    solved, from_x, from_y = lax.optimization_barrier((solved, from_x, from_y))
    parts_x = products([solved] + from_x, cross, 0)
    back_x = [lax.ppermute(part, "obs", steps_along(2, -d)) for part, d in zip(parts_x[1:], (2, 1, 3))]
    parts_y = products([solved] + from_y, cross, 1)
    back_y = [lax.ppermute(part, "obs", steps_along(0, -d)) for part, d in zip(parts_y[1:], (2, 1, 3))]
    out = downdate([at_x, 4 + at_y], [parts_x[0], parts_y[0]], cov_slab)
    out = downdate([(at_x + d) % 4 for d in (2, 1, 3)], back_x, cov_slab, out)
    return downdate([4 + (at_y + d) % 4 for d in (2, 1, 3)], back_y, cov_slab, out)


def solution(mesh):
    placed = (
        P("vox", "obs"),
        P("vox", "obs"),
        P("obs", None),
        P("obs", None),
        P("obs"),
        P("obs", None),
    )
    return jax.shard_map(
        shards, mesh=mesh, in_specs=placed, out_specs=P("vox", "obs"), check_vma=False
    )
```
